512 devices in a mesh: dp: 512 (over x, z, y, core).
Axes of the slice: x: 4, y: 8, z: 8, core: 2. Of those that a mesh axis runs over, the one named last changes fastest.
Arguments:
- sketch: bfloat16 [262144, 2048], P('dp'), may hold values from -5 to 5
- lanczos_basis: float32 [8, 262144], P(None, 'dp'), may hold values from -9 to 9
Outputs:
- gram_rows: bfloat16 [262144, 2560], P('dp')
- next_vector: float32 [262144], P('dp')
- coefficients: float32 [9], replicated
The draws below stay inside these ranges and needn't reach their ends.
All inputs are finite; a program needn't handle non-finite values.
Results may differ from the reference program's by a relative error of at most 0.0042.
Values may be sent and summed in bfloat16 or wider, within the bound.
No kernel may reach another device: no remote copies, remote signals or barrier semaphores. Data moves between devices by JAX's collectives and lax.ppermute only.
A program may use at most 64 MiB of HBM per device.

```python
import jax
import jax.numpy as jnp
from jax import lax

K = 2048
E_DEV = 512
M = 8
NTOT = 262144
N_DP = 512


def log_spread(key, shape, low, high):
    return jnp.exp(jax.random.uniform(key, shape, jnp.float32, jnp.log(low), jnp.log(high)))


def draw_sketch(key, part):
    key = jax.random.fold_in(key, 1)
    key_base, key_rows, key_cols = jax.random.split(key, 3)
    row_scale = log_spread(key_rows, (NTOT, 1), 0.3, 3.0)
    col_scale = log_spread(key_cols, (1, K), 0.3, 3.0) / 1.4
    base = jax.random.truncated_normal(key_base, -4.0, 4.0, (NTOT, K), jnp.float32)
    values = base * row_scale * col_scale
    return (values / jnp.sqrt(1.0 * K)).astype(jnp.bfloat16)


def draw_lanczos_basis(key, part):
    key = jax.random.fold_in(key, 2)
    key_common, key_own = jax.random.split(key, 2)
    ramp = 0.5 + jnp.arange(NTOT, dtype=jnp.float32) / NTOT
    common = jax.random.truncated_normal(key_common, -4.0, 4.0, (1, NTOT), jnp.float32)
    own_part = jax.random.truncated_normal(key_own, -4.0, 4.0, (M, NTOT), jnp.float32)
    values = 0.6 * common + 0.8 * own_part
    return (values * ramp[None, :]).astype(jnp.float32)


def setup_inputs(seed: int = 0) -> dict:
    splits = jax.random.split(jax.random.key(seed), 3)
    sketch = draw_sketch(jax.random.fold_in(splits[2], 71), 0)
    lanczos_basis = draw_lanczos_basis(jax.random.fold_in(splits[2], 71), 0)
    return {"sketch": sketch, "lanczos_basis": lanczos_basis}


def band_blocks(sketch):
    offsets = (1, N_DP // 4)

    def one_device(place):
        mine = lax.dynamic_slice_in_dim(sketch, place * E_DEV, E_DEV, 0).astype(jnp.float32)
        results = [jnp.dot(mine, mine.T, precision=lax.Precision.HIGHEST)]
        for offset in offsets:
            partner_start = ((place + offset) % N_DP * E_DEV).astype(jnp.int32)
            other = lax.dynamic_slice_in_dim(sketch, partner_start, E_DEV, 0).astype(jnp.float32)
            results.append(jnp.dot(mine, other.T, precision=lax.Precision.HIGHEST))
        return tuple((item.astype(jnp.bfloat16) for item in results))
    return lax.map(one_device, jnp.arange(N_DP, dtype=jnp.int32))

def apply_band(blocks, vectors, shift):
    partner_vec = jnp.roll(vectors, -shift, axis=0)
    return jnp.einsum('pij,pj->pi', blocks.astype(jnp.float32), partner_vec, precision=lax.Precision.HIGHEST)

def reference(sketch, lanczos_basis):
    first_off = 1
    second_off = N_DP // 4
    own_blocks, ahead_one, ahead_two = band_blocks(sketch)
    behind_one = jnp.swapaxes(jnp.roll(ahead_one, first_off, axis=0), 1, 2)
    behind_two = jnp.swapaxes(jnp.roll(ahead_two, second_off, axis=0), 1, 2)
    gram = jnp.concatenate([own_blocks, ahead_one, behind_one, ahead_two, behind_two], axis=2)
    gram_rows = gram.reshape(NTOT, 5 * E_DEV)
    vectors = lanczos_basis[M - 1].astype(jnp.bfloat16).astype(jnp.float32).reshape(N_DP, E_DEV)
    image_vec = apply_band(own_blocks, vectors, 0)
    image_vec = image_vec + apply_band(ahead_one, vectors, first_off) + apply_band(behind_one, vectors, -first_off)
    image_vec = image_vec + apply_band(ahead_two, vectors, second_off) + apply_band(behind_two, vectors, -second_off)
    image_vec = image_vec.reshape(NTOT)
    coeffs = jnp.dot(lanczos_basis, image_vec, precision=lax.Precision.HIGHEST) / NTOT
    remainder = image_vec - jnp.dot(coeffs, lanczos_basis, precision=lax.Precision.HIGHEST)
    beta_value = jnp.sqrt(jnp.sum(remainder * remainder) / NTOT + 1e-06)
    next_vector = remainder / beta_value
    coefficients = jnp.concatenate([coeffs, beta_value[None]])
    return (gram_rows, next_vector, coefficients)
```

```python
import functools

import jax
import jax.numpy as jnp
import numpy as np
from jax import lax
from jax.experimental import pallas as pl
from jax.experimental.pallas import tpu as pltpu
from jax.sharding import Mesh
from jax.sharding import PartitionSpec as P

AXES = ("x", "z", "y", "core")
SIZES = (4, 8, 8, 2)
FIRST_GROUP = ("z", "core")
SECOND_GROUP = ("x", "y")
BANDS = 5
VMEM_BYTES = 40 * 1024 * 1024
F32 = jnp.float32
BF16 = jnp.bfloat16


def dot_last(left, right, precision=None):
    return lax.dot_general(
        left, right, (((1,), (1,)), ((), ())), preferred_element_type=F32, precision=precision
    )


def params(**more):
    return pltpu.CompilerParams(vmem_limit_bytes=VMEM_BYTES, **more)


def whole(memory_space=pltpu.VMEM):
    return pl.BlockSpec(memory_space=memory_space)


def sketch_image_kernel(sketch_ref, basis_ref, u_ref):
    last = basis_ref.shape[0] - 1
    current = basis_ref[last : last + 1, :].astype(BF16)
    rows = jnp.broadcast_to(current, (16, current.shape[1]))
    product = jnp.dot(rows, sketch_ref[...], preferred_element_type=F32)
    u_ref[...] = product[0:1, :]


def sketch_image(sketch, basis):
    return pl.pallas_call(
        sketch_image_kernel,
        out_shape=jax.ShapeDtypeStruct((1, sketch.shape[1]), F32),
        in_specs=[whole(), whole()],
        out_specs=whole(),
        compiler_params=params(),
        cost_estimate=pl.CostEstimate(flops=2 * sketch.size, bytes_accessed=2 * sketch.size, transcendentals=0),
    )(sketch, basis)


def own_block_kernel(sketch_ref, basis_ref, rows_ref, own_image_ref):
    last = basis_ref.shape[0] - 1
    current = basis_ref[last : last + 1, :].astype(BF16)
    block = dot_last(sketch_ref[...], sketch_ref[...]).astype(BF16)
    rows_ref[...] = block
    vec = jnp.broadcast_to(current, (16, current.shape[1]))
    own_image_ref[...] = dot_last(vec, block)[0:1, :]


def own_block(sketch, basis):
    n, k = sketch.shape
    return pl.pallas_call(
        own_block_kernel,
        grid=(1,),
        out_shape=(
            jax.ShapeDtypeStruct((n, BANDS * n), BF16),
            jax.ShapeDtypeStruct((1, n), F32),
        ),
        in_specs=[
            pl.BlockSpec((n, k), lambda i: (0, 0)),
            pl.BlockSpec(basis.shape, lambda i: (0, 0)),
        ],
        out_specs=(
            pl.BlockSpec((n, n), lambda i: (0, 0)),
            pl.BlockSpec((1, n), lambda i: (0, 0)),
        ),
        compiler_params=params(),
        cost_estimate=pl.CostEstimate(flops=2 * n * n * k, bytes_accessed=2 * n * k, transcendentals=0),
    )(sketch, basis)


def image_kernel(sketch_ref, basis_ref, own_ref, a_ref, b_ref, c_ref, d_ref, image_ref, sums_ref):
    total = (a_ref[...] + b_ref[...]) + (c_ref[...] + d_ref[...])
    high = total.astype(BF16).astype(F32)
    rest = total - high
    middle = rest.astype(BF16).astype(F32)
    low = rest - middle
    row = lax.broadcasted_iota(jnp.int32, (16, total.shape[1]), 0)
    parts = jnp.where(row == 0, high, jnp.where(row == 1, middle, jnp.where(row == 2, low, 0.0)))
    product = dot_last(parts.astype(BF16), sketch_ref[...])
    image = (product[2:3, :] + product[1:2, :]) + product[0:1, :] + own_ref[...]
    image_ref[...] = image
    basis = basis_ref[...]
    m, n = basis.shape
    place = lax.broadcasted_iota(jnp.int32, (128 - m, n), 0)
    right = jnp.concatenate([basis, jnp.where(place == 0, image, 0.0)], axis=0)
    products = dot_last(basis, right, precision=lax.Precision.HIGHEST)
    norm = jnp.sum(image * image)
    lane = lax.broadcasted_iota(jnp.int32, products.shape, 1)
    sums_ref[...] = jnp.where(lane == m + 1, norm, products)


def image_and_sums(sketch, basis, own_image, parts):
    n, k = sketch.shape
    return pl.pallas_call(
        image_kernel,
        out_shape=(
            jax.ShapeDtypeStruct((1, n), F32),
            jax.ShapeDtypeStruct((basis.shape[0], 128), F32),
        ),
        in_specs=[whole()] * 7,
        out_specs=(whole(), whole()),
        compiler_params=params(),
        cost_estimate=pl.CostEstimate(flops=2 * n * k * 16, bytes_accessed=2 * n * k, transcendentals=0),
    )(sketch, basis, own_image, *parts)


def pair_kernel(column_ref, sketch_ref, other_ref, rows_in_ref, rows_ref, back_ref):
    del column_ref, rows_in_ref
    rows_ref[...] = dot_last(sketch_ref[...], other_ref[...]).astype(BF16)
    back_ref[...] = dot_last(other_ref[...], sketch_ref[...]).astype(BF16)


def pair_blocks(column, sketch, other, rows):
    n, k = sketch.shape
    return pl.pallas_call(
        pair_kernel,
        grid_spec=pltpu.PrefetchScalarGridSpec(
            num_scalar_prefetch=1,
            grid=(1,),
            in_specs=[
                pl.BlockSpec((n, k), lambda i, c: (0, 0)),
                pl.BlockSpec((n, k), lambda i, c: (0, 0)),
                pl.BlockSpec(memory_space=pl.ANY),
            ],
            out_specs=(
                pl.BlockSpec((n, n), lambda i, c: (0, c[0])),
                pl.BlockSpec((n, n), lambda i, c: (0, 0)),
            ),
        ),
        out_shape=(
            jax.ShapeDtypeStruct(rows.shape, rows.dtype),
            jax.ShapeDtypeStruct((n, n), BF16),
        ),
        input_output_aliases={3: 0},
        compiler_params=params(),
        cost_estimate=pl.CostEstimate(flops=4 * n * n * k, bytes_accessed=4 * n * k, transcendentals=0),
    )(column, sketch, other, rows)


def place_kernel(column_ref, block_ref, rows_in_ref, rows_ref):
    del column_ref, rows_in_ref
    rows_ref[...] = block_ref[...]


def place_block(column, block, rows):
    n = block.shape[0]
    return pl.pallas_call(
        place_kernel,
        grid_spec=pltpu.PrefetchScalarGridSpec(
            num_scalar_prefetch=1,
            grid=(1,),
            in_specs=[
                pl.BlockSpec((n, n), lambda i, c: (0, 0)),
                pl.BlockSpec(memory_space=pl.ANY),
            ],
            out_specs=pl.BlockSpec((n, n), lambda i, c: (0, c[0])),
        ),
        out_shape=jax.ShapeDtypeStruct(rows.shape, rows.dtype),
        input_output_aliases={2: 0},
        compiler_params=params(),
        cost_estimate=pl.CostEstimate(flops=0, bytes_accessed=4 * n * n, transcendentals=0),
    )(column, block, rows)


def finish_kernel(count, sums_ref, basis_ref, image_ref, left_ref, stats_ref):
    sums = jnp.sum(sums_ref[...], axis=0)
    basis = basis_ref[...]
    m = basis.shape[0]
    row = lax.broadcasted_iota(jnp.int32, sums.shape, 0)
    lane = lax.broadcasted_iota(jnp.int32, sums.shape, 1)
    inner = jnp.sum(jnp.where(lane == m, sums, 0.0), axis=1, keepdims=True)
    norm = jnp.sum(jnp.where((lane == m + 1) & (row == 0), sums, 0.0))
    coeffs = inner / count
    across = jnp.sum(jnp.where(lane == row, coeffs, 0.0), axis=0, keepdims=True)
    gram = jnp.where(lane < m, sums, 0.0)
    quadratic = jnp.sum(jnp.sum(coeffs * gram, axis=0, keepdims=True) * across)
    cross = jnp.sum(coeffs * inner)
    square = (norm - cross) + (quadratic - cross)
    left_ref[...] = image_ref[...] - jnp.sum(coeffs * basis, axis=0, keepdims=True)
    lane_row = lax.broadcasted_iota(jnp.int32, across.shape, 1)
    stats = jnp.where(lane_row == m, square, across)
    stats_ref[...] = jnp.where(lane_row == m + 1, norm, stats)


def finish(sums, basis, image, count):
    n = image.shape[1]
    return pl.pallas_call(
        functools.partial(finish_kernel, count),
        out_shape=(
            jax.ShapeDtypeStruct((1, n), F32),
            jax.ShapeDtypeStruct((1, 128), F32),
        ),
        in_specs=[whole()] * 3,
        out_specs=(whole(), whole()),
        compiler_params=params(),
    )(sums, basis, image)


def everyones(block, group):
    members = 1
    for name in group:
        members *= lax.axis_size(name)
    copies = jnp.broadcast_to(block[None], (members, *block.shape))
    return lax.all_to_all(copies, group, 0, 0, tiled=True)


def on_device(sketch, basis):
    devices = 1
    for name in AXES:
        devices *= lax.axis_size(name)
    stride = devices // 4
    total_rows = sketch.shape[0] * devices
    is_second = lax.axis_index("core")

    def move(block, source_of):
        return lax.ppermute(block, AXES, [(source_of(i) % devices, i) for i in range(devices)])

    u = sketch_image(sketch, basis)
    parts = [
        move(u, lambda i: i ^ 1),
        move(u, lambda i: i - 1 if i % 2 == 0 else i + 1),
        move(u, lambda i: i + stride),
        move(u, lambda i: i - stride),
    ]
    far = move(sketch, lambda i: i + stride if i % 2 == 0 else i - stride)
    near = move(sketch, lambda i: i + 1)
    rows, own_image = own_block(sketch, basis)
    image, sums = image_and_sums(sketch, basis, own_image, parts)
    sums = jnp.sum(everyones(sums, FIRST_GROUP), axis=0)
    sums = everyones(sums, SECOND_GROUP)

    one = jnp.ones((1,), jnp.int32)
    far_column = (3 + is_second).astype(jnp.int32)[None]
    rows, far_back = pair_blocks(far_column, sketch, far, rows)
    far_back = move(far_back, lambda i: i - stride if i % 2 == 0 else i + stride)
    rows, near_back = pair_blocks(one, sketch, near, rows)
    near_back = move(near_back, lambda i: i - 1)

    left, stats = finish(sums, basis, image, float(total_rows))
    m = basis.shape[0]
    square, norm = stats[0, m], stats[0, m + 1]
    square = lax.cond(
        square < 1e-3 * norm,
        lambda: lax.psum(jnp.sum(left * left), AXES),
        lambda: square,
    )
    beta = jnp.sqrt(square / total_rows + 1e-06)
    next_vector = left[0] / beta
    coefficients = jnp.concatenate([stats[0, :m], beta[None]])

    rows = place_block(7 - far_column, far_back, rows)
    rows = place_block(2 * one, near_back, rows)
    return rows, next_vector, coefficients


def solution(mesh):
    grid = Mesh(np.asarray(mesh.devices).reshape(SIZES), AXES)
    return jax.shard_map(
        on_device,
        mesh=grid,
        in_specs=(P(AXES, None), P(None, AXES)),
        out_specs=(P(AXES, None), P(AXES), P()),
        check_vma=False,
    )
```

```python
import functools

import jax
import jax.numpy as jnp
import numpy as np
from jax import lax
from jax.experimental import pallas as pl
from jax.experimental.pallas import tpu as pltpu
from jax.sharding import Mesh
from jax.sharding import PartitionSpec as P

AXES = ("x", "z", "y", "core")
SIZES = (4, 8, 8, 2)
FIRST_GROUP = ("z", "core")
SECOND_GROUP = ("x", "y")
BANDS = 5
VMEM_BYTES = 16 * 1024 * 1024
LOAD_VMEM_BYTES = 16 * 1024 * 1024
EXTRA = 16
F32 = jnp.float32
BF16 = jnp.bfloat16


def dot_last(left, right, precision=None):
    return lax.dot_general(
        left, right, (((1,), (1,)), ((), ())), preferred_element_type=F32, precision=precision
    )


def params(**more):
    return pltpu.CompilerParams(vmem_limit_bytes=VMEM_BYTES, **more)


def whole(memory_space=pltpu.VMEM):
    return pl.BlockSpec(memory_space=memory_space)


def shaped(shape, dtype=F32):
    return jax.ShapeDtypeStruct(shape, dtype)


def load_kernel(chunks, sketch_hbm, basis_ref, held_ref, u_ref, sems):
    last = basis_ref.shape[0] - 1
    rows, k = sketch_hbm.shape
    n = rows // chunks
    copies = []
    for i in range(chunks):
        piece = pl.ds(i * n, n)
        copies.append(pltpu.make_async_copy(sketch_hbm.at[piece], held_ref.at[piece], sems.at[i]))
        copies[i].start()
    current = jnp.broadcast_to(basis_ref[last : last + 1, :], (EXTRA, rows))
    held_ref[rows:, :] = jnp.concatenate([current, jnp.zeros((EXTRA, k - rows), F32)], axis=1).astype(BF16)
    total = None
    for i in range(chunks):
        copies[i].wait()
        part = jnp.dot(
            current[:, i * n : (i + 1) * n].astype(BF16),
            held_ref[i * n : (i + 1) * n, :],
            preferred_element_type=F32,
        )
        total = part if total is None else total + part
    u_ref[...] = total[0:1, :]


def load_and_project(sketch, basis):
    chunks = 4
    n, k = sketch.shape
    return pl.pallas_call(
        functools.partial(load_kernel, chunks),
        out_shape=(shaped((n + EXTRA, k), BF16), shaped((1, k))),
        in_specs=[whole(pltpu.HBM), whole()],
        out_specs=(whole(), whole()),
        scratch_shapes=[pltpu.SemaphoreType.DMA((chunks,))],
        compiler_params=pltpu.CompilerParams(vmem_limit_bytes=LOAD_VMEM_BYTES),
        cost_estimate=pl.CostEstimate(
            flops=2 * sketch.size, bytes_accessed=0, transcendentals=0
        ),
    )(sketch, basis)


def pass_kernel(*refs):
    del refs


def after(block, *tokens):
    return pl.pallas_call(
        pass_kernel,
        out_shape=shaped(block.shape, block.dtype),
        in_specs=[whole()] * (1 + len(tokens)),
        out_specs=whole(),
        input_output_aliases={0: 0},
        compiler_params=params(),
    )(block, *tokens)


def own_block_kernel(sketch_ref, basis_ref, rows_ref, own_image_ref, block_ref, sem):
    last = basis_ref.shape[0] - 1
    n = block_ref.shape[0]
    current = basis_ref[last : last + 1, :].astype(BF16)
    sketch = sketch_ref[:n, :]
    block = dot_last(sketch, sketch).astype(BF16)
    block_ref[...] = block
    copy = pltpu.make_async_copy(block_ref, rows_ref.at[:, pl.ds(0, n)], sem)
    copy.start()
    own_image_ref[...] = dot_last(jnp.broadcast_to(current, (16, n)), block)[0:1, :]
    copy.wait()


def own_block(sketch, basis):
    n, k = basis.shape[1], sketch.shape[1]
    return pl.pallas_call(
        own_block_kernel,
        out_shape=(shaped((n, BANDS * n), BF16), shaped((1, n))),
        in_specs=[whole(), whole()],
        out_specs=(whole(pl.ANY), whole()),
        scratch_shapes=[pltpu.VMEM((n, n), BF16), pltpu.SemaphoreType.DMA],
        compiler_params=params(),
        cost_estimate=pl.CostEstimate(
            flops=2 * n * n * k, bytes_accessed=2 * n * k, transcendentals=0
        ),
    )(sketch, basis)


def image_kernel(sketch_ref, mate_ref, basis_ref, own_ref, a_ref, b_ref, c_ref, image_ref, sums_ref):
    rows = own_ref.shape[1]
    mate_u = jnp.dot(mate_ref[rows:, :rows], mate_ref[:rows, :], preferred_element_type=F32)
    total = (a_ref[...] + b_ref[...]) + (c_ref[...] + mate_u[0:1, :])
    high = total.astype(BF16).astype(F32)
    rest = total - high
    middle = rest.astype(BF16).astype(F32)
    low = rest - middle
    row = lax.broadcasted_iota(jnp.int32, (16, total.shape[1]), 0)
    parts = jnp.where(row == 0, high, jnp.where(row == 1, middle, jnp.where(row == 2, low, 0.0)))
    product = dot_last(parts.astype(BF16), sketch_ref[:rows, :])
    image = (product[2:3, :] + product[1:2, :]) + product[0:1, :] + own_ref[...]
    image_ref[...] = image
    basis = basis_ref[...]
    m, n = basis.shape
    place = lax.broadcasted_iota(jnp.int32, (m, n), 0)
    right = jnp.concatenate([basis, jnp.where(place == 0, image, 0.0)] * m, axis=0)
    products = dot_last(basis, right, precision=lax.Precision.HIGHEST)
    norm = jnp.sum(image * image)
    lane = lax.broadcasted_iota(jnp.int32, products.shape, 1)
    line = lax.broadcasted_iota(jnp.int32, products.shape, 0)
    kept = jnp.where((lane // (2 * m)) == line, products, 0.0)
    packed = jnp.sum(kept, axis=0, keepdims=True)
    packed = jnp.where(lane[0:1, :] == m + 1, norm, packed)
    sums_ref[...] = jnp.broadcast_to(packed, sums_ref.shape)


def image_and_sums(sketch, mate, basis, own_image, parts, copies):
    n, k = basis.shape[1], sketch.shape[1]
    return pl.pallas_call(
        image_kernel,
        out_shape=(shaped((1, n)), shaped((copies, 16 * basis.shape[0]))),
        in_specs=[whole()] * 7,
        out_specs=(whole(), whole()),
        compiler_params=params(),
        cost_estimate=pl.CostEstimate(
            flops=2 * n * k * 16, bytes_accessed=2 * n * k, transcendentals=0
        ),
    )(sketch, mate, basis, own_image, *parts)


def add_kernel(rows_ref, copies_ref):
    total = jnp.sum(rows_ref[...], axis=0, keepdims=True)
    copies_ref[...] = jnp.broadcast_to(total, copies_ref.shape)


def add_and_copy(rows, copies):
    return pl.pallas_call(
        add_kernel,
        out_shape=shaped((copies, rows.shape[1])),
        in_specs=[whole()],
        out_specs=whole(),
        compiler_params=params(),
    )(rows)


def plane_rank():
    rank, size = 0, 1
    for name in AXES[1:]:
        rank = rank * lax.axis_size(name) + lax.axis_index(name)
        size = size * lax.axis_size(name)
    return rank, size - 1


def corner_kernel(far_ref, near_ref, token_ref, corner_ref):
    del token_ref
    n = corner_ref.shape[0]
    rank, last = plane_rank()

    @pl.when((rank == 0) | (rank == last))
    def _():
        corner_ref[...] = dot_last(near_ref[:n, :], far_ref[:n, :]).astype(BF16)


def corner_block(far, near, token, n):
    return pl.pallas_call(
        corner_kernel,
        out_shape=shaped((n, n), BF16),
        in_specs=[whole()] * 3,
        out_specs=whole(),
        compiler_params=params(),
    )(far, near, token)


def far_kernel(sketch_ref, far_ref, token_ref, back_ref, block_ref):
    del token_ref
    n = back_ref.shape[0]
    back = dot_last(far_ref[:n, :], sketch_ref[:n, :]).astype(BF16)
    back_ref[...] = back
    block_ref[...] = back.T


def far_blocks(sketch, far, token, n):
    k = sketch.shape[1]
    block = shaped((n, n), BF16)
    return pl.pallas_call(
        far_kernel,
        out_shape=(block, block),
        in_specs=[whole()] * 3,
        out_specs=(whole(), whole()),
        compiler_params=params(),
        cost_estimate=pl.CostEstimate(
            flops=2 * n * n * k, bytes_accessed=4 * n * k, transcendentals=0
        ),
    )(sketch, far, token)


def column_copy(block_ref, rows_ref, column, sem):
    n = block_ref.shape[0]
    start = column * n if isinstance(column, int) else pl.multiple_of(column * n, n)
    return pltpu.make_async_copy(block_ref, rows_ref.at[:, pl.ds(start, n)], sem)


def pairs_kernel(
    sketch_ref, mate_ref, near_ref, far_ref, rows_in_ref, rows_ref, token_ref, blocks_ref, sems
):
    del rows_in_ref
    token_ref[...] = jnp.zeros_like(token_ref)
    n = far_ref.shape[0]
    core = lax.axis_index("core")
    copies = [column_copy(far_ref, rows_ref, 3 + core, sems.at[0])]
    copies[0].start()
    for i, (other_ref, column) in enumerate(((mate_ref, 1 + core), (near_ref, 2 - core))):
        blocks_ref[i] = dot_last(sketch_ref[:n, :], other_ref[:n, :]).astype(BF16)
        copies.append(column_copy(blocks_ref.at[i], rows_ref, column, sems.at[1 + i]))
        copies[-1].start()
    for copy in copies:
        copy.wait()


def pair_blocks(sketch, mate, near, far, rows):
    n, k = far.shape[0], sketch.shape[1]
    return pl.pallas_call(
        pairs_kernel,
        out_shape=(shaped(rows.shape, rows.dtype), shaped((8, 128))),
        in_specs=[whole()] * 4 + [whole(pl.ANY)],
        out_specs=(whole(pl.ANY), whole()),
        scratch_shapes=[pltpu.VMEM((2, n, n), BF16), pltpu.SemaphoreType.DMA((3,))],
        input_output_aliases={4: 0},
        compiler_params=params(),
        cost_estimate=pl.CostEstimate(
            flops=4 * n * n * k, bytes_accessed=4 * n * k, transcendentals=0
        ),
    )(sketch, mate, near, far, rows)


def place_corner_kernel(corner_ref, rows_in_ref, rows_ref, sem):
    del rows_in_ref
    rank, last = plane_rank()

    @pl.when((rank == 0) | (rank == last))
    def _():
        copy = column_copy(corner_ref, rows_ref, jnp.where(rank == 0, 2, 1), sem)
        copy.start()
        copy.wait()


def place_far_kernel(block_ref, rows_in_ref, rows_ref, sem):
    del rows_in_ref
    copy = column_copy(block_ref, rows_ref, 4 - lax.axis_index("core"), sem)
    copy.start()
    copy.wait()


def place(kernel, block, rows):
    n = block.shape[0]
    return pl.pallas_call(
        kernel,
        out_shape=shaped(rows.shape, rows.dtype),
        in_specs=[whole(), whole(pl.ANY)],
        out_specs=whole(pl.ANY),
        scratch_shapes=[pltpu.SemaphoreType.DMA],
        input_output_aliases={1: 0},
        compiler_params=params(),
        cost_estimate=pl.CostEstimate(flops=0, bytes_accessed=4 * n * n, transcendentals=0),
    )(block, rows)


def finish_kernel(count, sums_ref, basis_ref, image_ref, token_ref, left_ref, next_ref, stats_ref, lost_ref):
    del token_ref
    sums = jnp.sum(sums_ref[...], axis=0, keepdims=True)
    basis = basis_ref[...]
    m = basis.shape[0]
    shape = (m, sums.shape[1])
    line = lax.broadcasted_iota(jnp.int32, shape, 0)
    lane = lax.broadcasted_iota(jnp.int32, shape, 1)
    major, minor = lane // (2 * m), lane % (2 * m)
    spread = jnp.broadcast_to(sums, shape)
    inner = jnp.sum(jnp.where((major == line) & (minor == m), spread, 0.0), axis=1, keepdims=True)
    norm = jnp.sum(jnp.where(lane[0:1, :] == m + 1, sums, 0.0), axis=1, keepdims=True)
    coeffs = inner / count
    by_major = jnp.sum(jnp.where(major == line, coeffs, 0.0), axis=0, keepdims=True)
    by_minor = jnp.sum(jnp.where(minor == line, coeffs, 0.0), axis=0, keepdims=True)
    by_lane = jnp.sum(jnp.where(lane == line, coeffs, 0.0), axis=0, keepdims=True)
    quadratic = jnp.sum(sums * by_major * by_minor, axis=1, keepdims=True)
    cross = jnp.sum(coeffs * inner, axis=0, keepdims=True)
    square = (norm - cross) + (quadratic - cross)
    beta = jnp.sqrt(jnp.maximum(square, 0.0) / count + 1e-06)
    left = image_ref[...] - jnp.sum(coeffs * basis, axis=0, keepdims=True)
    left_ref[...] = left
    next_ref[...] = left / beta
    stats_ref[...] = jnp.where(lane[0:1, :] == m, beta, by_lane)
    largest = norm + cross + jnp.abs(quadratic)
    lost_ref[0] = jnp.max(jnp.where(square < 1e-3 * largest, 1.0, 0.0)).astype(jnp.int32)


def finish(sums, basis, image, count, token):
    row = shaped(image.shape)
    return pl.pallas_call(
        functools.partial(finish_kernel, count),
        out_shape=(row, row, shaped((1, 128)), shaped((1,), jnp.int32)),
        in_specs=[whole()] * 4,
        out_specs=(whole(), whole(), whole(), whole(pltpu.SMEM)),
        compiler_params=params(),
    )(sums, basis, image, token)


def group_size(group):
    members = 1
    for name in group:
        members *= lax.axis_size(name)
    return members


def on_device(sketch, basis):
    devices = group_size(AXES)
    stride = devices // SIZES[0]
    total_rows = basis.shape[1] * devices

    def move(block, source_of):
        return lax.ppermute(block, AXES, [(source_of(i) % devices, i) for i in range(devices)])

    def trade(rows, group):
        return lax.all_to_all(rows, group, 0, 0, tiled=True)

    rows_each = sketch.shape[0]
    sketch, u = load_and_project(sketch, basis)
    mate = move(sketch, lambda i: i ^ 1)
    parts = (
        move(u, lambda i: i - 1 if i % 2 == 0 else i + 1),
        move(u, lambda i: i + stride if (i // stride) % 2 == 0 else i - stride),
        move(u, lambda i: i - stride if (i // stride) % 2 == 0 else i + stride),
    )
    sketch = after(sketch, mate, *parts)

    def in_plane(i, step):
        return i // stride * stride + (i + step) % stride

    near = move(sketch, lambda i: in_plane(i, -1 if i % 2 == 0 else 1))
    far = move(sketch, lambda i: i + stride if i % 2 == 0 else i - stride)
    rows, own_image = own_block(sketch, basis)
    image, sums = image_and_sums(sketch, mate, basis, own_image, parts, group_size(FIRST_GROUP))
    sums = add_and_copy(trade(sums, FIRST_GROUP), group_size(SECOND_GROUP))
    sums = trade(sums, SECOND_GROUP)

    corner = corner_block(far, near, sums, rows_each)
    far_back, far_block = far_blocks(sketch, far, corner, rows_each)
    corners = [(i, i + stride - 1) for i in range(0, devices, stride)]
    corner = lax.ppermute(corner, AXES, corners + [(j, i) for i, j in corners])
    far_back = move(far_back, lambda i: i - stride if i % 2 == 0 else i + stride)
    rows, token = pair_blocks(sketch, mate, near, far_block, rows)
    left, next_vector, stats, lost = finish(sums, basis, image, float(total_rows), token)

    m = basis.shape[0]

    def from_sums():
        return next_vector[0], stats[0, : m + 1]

    def from_vector():
        square = lax.psum(jnp.sum(left * left), AXES)
        beta = jnp.sqrt(square / total_rows + 1e-06)
        return left[0] / beta, jnp.concatenate([stats[0, :m], beta[None]])

    next_vector, coefficients = lax.cond(lost[0] != 0, from_vector, from_sums)
    rows = place(place_corner_kernel, corner, rows)
    rows = place(place_far_kernel, far_back, rows)
    return rows, next_vector, coefficients


def solution(mesh):
    grid = Mesh(np.asarray(mesh.devices).reshape(SIZES), AXES)
    return jax.shard_map(
        on_device,
        mesh=grid,
        in_specs=(P(AXES, None), P(None, AXES)),
        out_specs=(P(AXES, None), P(AXES), P()),
        check_vma=False,
    )
```

```python
import functools

import jax
import jax.numpy as jnp
import numpy as np
from jax import lax
from jax.experimental import pallas as pl
from jax.experimental.pallas import tpu as pltpu
from jax.sharding import Mesh
from jax.sharding import PartitionSpec as P

AXES = ("x", "z", "y", "core")
SIZES = (4, 8, 8, 2)
FIRST_GROUP = ("z", "core")
SECOND_GROUP = ("x", "y")
BANDS = 5
VMEM_BYTES = 16 * 1024 * 1024
LOAD_VMEM_BYTES = 16 * 1024 * 1024
EXTRA = 16
F32 = jnp.float32
BF16 = jnp.bfloat16


def dot_last(left, right, precision=None):
    return lax.dot_general(
        left, right, (((1,), (1,)), ((), ())), preferred_element_type=F32, precision=precision
    )


def params(**more):
    return pltpu.CompilerParams(vmem_limit_bytes=VMEM_BYTES, **more)


def whole(memory_space=pltpu.VMEM):
    return pl.BlockSpec(memory_space=memory_space)


def shaped(shape, dtype=F32):
    return jax.ShapeDtypeStruct(shape, dtype)


def load_kernel(chunks, sketch_hbm, basis_hbm, held_ref, u_ref, basis_ref, sems):
    last = basis_ref.shape[0] - 1
    rows, k = sketch_hbm.shape
    n = rows // chunks
    basis_copy = pltpu.make_async_copy(basis_hbm, basis_ref, sems.at[chunks])
    basis_copy.start()
    copies = []
    for i in range(chunks):
        piece = pl.ds(i * n, n)
        copies.append(pltpu.make_async_copy(sketch_hbm.at[piece], held_ref.at[piece], sems.at[i]))
        copies[i].start()
    basis_copy.wait()
    current = jnp.broadcast_to(basis_ref[last : last + 1, :], (EXTRA, rows))
    held_ref[rows:, :] = jnp.concatenate([current, jnp.zeros((EXTRA, k - rows), F32)], axis=1).astype(BF16)
    total = None
    for i in range(chunks):
        copies[i].wait()
        part = jnp.dot(
            current[:, i * n : (i + 1) * n].astype(BF16),
            held_ref[i * n : (i + 1) * n, :],
            preferred_element_type=F32,
        )
        total = part if total is None else total + part
    u_ref[...] = total[0:1, :]


def load_and_project(sketch, basis):
    chunks = 4
    n, k = sketch.shape
    return pl.pallas_call(
        functools.partial(load_kernel, chunks),
        out_shape=(shaped((n + EXTRA, k), BF16), shaped((1, k)), shaped(basis.shape)),
        in_specs=[whole(pltpu.HBM), whole(pltpu.HBM)],
        out_specs=(whole(), whole(), whole()),
        scratch_shapes=[pltpu.SemaphoreType.DMA((chunks + 1,))],
        compiler_params=pltpu.CompilerParams(vmem_limit_bytes=LOAD_VMEM_BYTES),
        cost_estimate=pl.CostEstimate(
            flops=2 * sketch.size, bytes_accessed=0, transcendentals=0
        ),
    )(sketch, basis)


def mate_kernel(mate_ref, u_ref):
    n = mate_ref.shape[0] - EXTRA
    product = jnp.dot(mate_ref[n:, :n], mate_ref[:n, :], preferred_element_type=F32)
    u_ref[...] = product[0:1, :]


def mate_projection(mate):
    return pl.pallas_call(
        mate_kernel,
        out_shape=shaped((1, mate.shape[1])),
        in_specs=[whole()],
        out_specs=whole(),
        compiler_params=params(),
        cost_estimate=pl.CostEstimate(flops=2 * mate.size, bytes_accessed=2 * mate.size, transcendentals=0),
    )(mate)


def own_block_kernel(sketch_ref, basis_ref, rows_ref, own_image_ref, block_ref, sem):
    last = basis_ref.shape[0] - 1
    n = block_ref.shape[0]
    current = basis_ref[last : last + 1, :].astype(BF16)
    sketch = sketch_ref[:n, :]
    block = dot_last(sketch, sketch).astype(BF16)
    block_ref[...] = block
    copy = pltpu.make_async_copy(block_ref, rows_ref.at[:, pl.ds(0, n)], sem)
    copy.start()
    own_image_ref[...] = dot_last(jnp.broadcast_to(current, (16, n)), block)[0:1, :]
    copy.wait()


def own_block(sketch, basis):
    n, k = basis.shape[1], sketch.shape[1]
    return pl.pallas_call(
        own_block_kernel,
        out_shape=(shaped((n, BANDS * n), BF16), shaped((1, n))),
        in_specs=[whole(), whole()],
        out_specs=(whole(pl.ANY), whole()),
        scratch_shapes=[pltpu.VMEM((n, n), BF16), pltpu.SemaphoreType.DMA],
        compiler_params=params(),
        cost_estimate=pl.CostEstimate(
            flops=2 * n * n * k, bytes_accessed=2 * n * k, transcendentals=0
        ),
    )(sketch, basis)


def image_kernel(sketch_ref, basis_ref, own_ref, a_ref, b_ref, c_ref, d_ref, image_ref, sums_ref):
    rows = own_ref.shape[1]
    total = (a_ref[...] + b_ref[...]) + (c_ref[...] + d_ref[...])
    high = total.astype(BF16).astype(F32)
    rest = total - high
    middle = rest.astype(BF16).astype(F32)
    low = rest - middle
    row = lax.broadcasted_iota(jnp.int32, (16, total.shape[1]), 0)
    parts = jnp.where(row == 0, high, jnp.where(row == 1, middle, jnp.where(row == 2, low, 0.0)))
    product = dot_last(parts.astype(BF16), sketch_ref[:rows, :])
    image = (product[2:3, :] + product[1:2, :]) + product[0:1, :] + own_ref[...]
    image_ref[...] = image
    basis = basis_ref[...]
    m, n = basis.shape
    place = lax.broadcasted_iota(jnp.int32, (m, n), 0)
    right = jnp.concatenate([basis, jnp.where(place == 0, image, 0.0)] * m, axis=0)
    products = dot_last(basis, right, precision=lax.Precision.HIGHEST)
    norm = jnp.sum(image * image)
    lane = lax.broadcasted_iota(jnp.int32, products.shape, 1)
    line = lax.broadcasted_iota(jnp.int32, products.shape, 0)
    kept = jnp.where((lane // (2 * m)) == line, products, 0.0)
    packed = jnp.sum(kept, axis=0, keepdims=True)
    packed = jnp.where(lane[0:1, :] == m + 1, norm, packed)
    sums_ref[...] = jnp.broadcast_to(packed, sums_ref.shape)


def image_and_sums(sketch, basis, own_image, parts, copies):
    n, k = basis.shape[1], sketch.shape[1]
    return pl.pallas_call(
        image_kernel,
        out_shape=(shaped((1, n)), shaped((copies, 16 * basis.shape[0]))),
        in_specs=[whole()] * 7,
        out_specs=(whole(), whole()),
        compiler_params=params(),
        cost_estimate=pl.CostEstimate(
            flops=2 * n * k * 16, bytes_accessed=2 * n * k, transcendentals=0
        ),
    )(sketch, basis, own_image, *parts)


def add_kernel(rows_ref, copies_ref):
    total = jnp.sum(rows_ref[...], axis=0, keepdims=True)
    copies_ref[...] = jnp.broadcast_to(total, copies_ref.shape)


def add_and_copy(rows, copies):
    return pl.pallas_call(
        add_kernel,
        out_shape=shaped((copies, rows.shape[1])),
        in_specs=[whole()],
        out_specs=whole(),
        compiler_params=params(),
    )(rows)


def plane_rank():
    rank, size = 0, 1
    for name in AXES[1:]:
        rank = rank * lax.axis_size(name) + lax.axis_index(name)
        size = size * lax.axis_size(name)
    return rank, size - 1


def corner_kernel(far_ref, near_ref, token_ref, corner_ref):
    del token_ref
    rank, last = plane_rank()

    @pl.when((rank == 0) | (rank == last))
    def _():
        corner_ref[...] = dot_last(far_ref[...], near_ref[...]).astype(BF16)


def corner_block(far, near, token, n):
    return pl.pallas_call(
        corner_kernel,
        out_shape=shaped((n, n), BF16),
        in_specs=[whole()] * 3,
        out_specs=whole(),
        compiler_params=params(),
    )(far, near, token)


def far_kernel(sketch_ref, far_ref, token_ref, back_ref, block_ref):
    del token_ref
    n = back_ref.shape[0]
    back = dot_last(far_ref[...], sketch_ref[:n, :]).astype(BF16)
    back_ref[...] = back
    block_ref[...] = back.T


def far_blocks(sketch, far, token, n):
    k = sketch.shape[1]
    block = shaped((n, n), BF16)
    return pl.pallas_call(
        far_kernel,
        out_shape=(block, block),
        in_specs=[whole()] * 3,
        out_specs=(whole(), whole()),
        compiler_params=params(),
        cost_estimate=pl.CostEstimate(
            flops=2 * n * n * k, bytes_accessed=4 * n * k, transcendentals=0
        ),
    )(sketch, far, token)


def column_copy(block_ref, rows_ref, column, sem):
    n = block_ref.shape[0]
    start = column * n if isinstance(column, int) else pl.multiple_of(column * n, n)
    return pltpu.make_async_copy(block_ref, rows_ref.at[:, pl.ds(start, n)], sem)


def pairs_kernel(
    sketch_ref, mate_ref, near_ref, far_ref, back_ref, corner_ref, sums_ref, rows_in_ref,
    rows_ref, token_ref, blocks_ref, sems,
):
    del sums_ref, rows_in_ref
    token_ref[...] = jnp.zeros_like(token_ref)
    n = far_ref.shape[0]
    core = lax.axis_index("core")
    rank, last = plane_rank()
    copies = [
        column_copy(far_ref, rows_ref, 3 + core, sems.at[0]),
        column_copy(back_ref, rows_ref, 4 - core, sems.at[1]),
    ]
    for copy in copies:
        copy.start()
    blocks_ref[0] = dot_last(sketch_ref[:n, :], mate_ref[:n, :]).astype(BF16)
    copies.append(column_copy(blocks_ref.at[0], rows_ref, 1 + core, sems.at[2]))
    copies[-1].start()
    blocks_ref[1] = dot_last(sketch_ref[:n, :], near_ref[...]).astype(BF16)

    @pl.when((rank == 0) | (rank == last))
    def _():
        blocks_ref[1] = corner_ref[...]

    copies.append(column_copy(blocks_ref.at[1], rows_ref, 2 - core, sems.at[3]))
    copies[-1].start()
    for copy in copies:
        copy.wait()


def pair_blocks(sketch, mate, near, far, back, corner, sums, rows):
    n, k = near.shape
    return pl.pallas_call(
        pairs_kernel,
        out_shape=(shaped(rows.shape, rows.dtype), shaped((8, 128))),
        in_specs=[whole()] * 7 + [whole(pl.ANY)],
        out_specs=(whole(pl.ANY), whole()),
        scratch_shapes=[pltpu.VMEM((2, n, n), BF16), pltpu.SemaphoreType.DMA((4,))],
        input_output_aliases={7: 0},
        compiler_params=params(),
        cost_estimate=pl.CostEstimate(
            flops=4 * n * n * k, bytes_accessed=4 * n * k, transcendentals=0
        ),
    )(sketch, mate, near, far, back, corner, sums, rows)


def finish_kernel(count, sums_ref, basis_ref, image_ref, token_ref, left_ref, next_ref, stats_ref, lost_ref):
    del token_ref
    sums = jnp.sum(sums_ref[...], axis=0, keepdims=True)
    basis = basis_ref[...]
    m = basis.shape[0]
    shape = (m, sums.shape[1])
    line = lax.broadcasted_iota(jnp.int32, shape, 0)
    lane = lax.broadcasted_iota(jnp.int32, shape, 1)
    major, minor = lane // (2 * m), lane % (2 * m)
    spread = jnp.broadcast_to(sums, shape)
    inner = jnp.sum(jnp.where((major == line) & (minor == m), spread, 0.0), axis=1, keepdims=True)
    norm = jnp.sum(jnp.where(lane[0:1, :] == m + 1, sums, 0.0), axis=1, keepdims=True)
    coeffs = inner / count
    by_major = jnp.sum(jnp.where(major == line, coeffs, 0.0), axis=0, keepdims=True)
    by_minor = jnp.sum(jnp.where(minor == line, coeffs, 0.0), axis=0, keepdims=True)
    by_lane = jnp.sum(jnp.where(lane == line, coeffs, 0.0), axis=0, keepdims=True)
    quadratic = jnp.sum(sums * by_major * by_minor, axis=1, keepdims=True)
    cross = jnp.sum(coeffs * inner, axis=0, keepdims=True)
    square = (norm - cross) + (quadratic - cross)
    beta = jnp.sqrt(jnp.maximum(square, 0.0) / count + 1e-06)
    left = image_ref[...] - jnp.sum(coeffs * basis, axis=0, keepdims=True)
    left_ref[...] = left
    next_ref[...] = left / beta
    stats_ref[...] = jnp.where(lane[0:1, :] == m, beta, by_lane)
    largest = norm + cross + jnp.abs(quadratic)
    lost_ref[0] = jnp.max(jnp.where(square < 1e-3 * largest, 1.0, 0.0)).astype(jnp.int32)


def finish(sums, basis, image, count, token):
    row = shaped(image.shape)
    return pl.pallas_call(
        functools.partial(finish_kernel, count),
        out_shape=(row, row, shaped((1, 128)), shaped((1,), jnp.int32)),
        in_specs=[whole()] * 4,
        out_specs=(whole(), whole(), whole(), whole(pltpu.SMEM)),
        compiler_params=params(),
    )(sums, basis, image, token)


def group_size(group):
    members = 1
    for name in group:
        members *= lax.axis_size(name)
    return members


def on_device(sketch, basis):
    devices = group_size(AXES)
    stride = devices // SIZES[0]
    total_rows = basis.shape[1] * devices

    def move(block, source_of):
        return lax.ppermute(block, AXES, [(source_of(i) % devices, i) for i in range(devices)])

    def trade(rows, group):
        return lax.all_to_all(rows, group, 0, 0, tiled=True)

    rows_each = sketch.shape[0]

    def in_plane(i, step):
        return i // stride * stride + (i + step) % stride

    far = move(sketch, lambda i: i + stride if i % 2 == 0 else i - stride)
    near = move(sketch, lambda i: in_plane(i, -1 if i % 2 == 0 else 1))
    stored = [pltpu.with_memory_space_constraint(array, pltpu.HBM) for array in (sketch, basis)]
    sketch, u, basis = load_and_project(*stored)
    mate = move(sketch, lambda i: i ^ 1)
    mate_u = mate_projection(mate)
    parts = (
        move(u, lambda i: i - stride if i % 2 == 0 else i + stride),
        move(mate_u, lambda i: i + stride + 1 if i % 2 == 0 else i - stride - 1),
        move(mate_u, lambda i: i - 2 if i % 2 == 0 else i + 2),
        mate_u,
    )
    rows, own_image = own_block(sketch, basis)
    image, sums = image_and_sums(sketch, basis, own_image, parts, group_size(FIRST_GROUP))
    sums = add_and_copy(trade(sums, FIRST_GROUP), group_size(SECOND_GROUP))
    corner = corner_block(far, near, sums, rows_each)
    far_back, far_block = far_blocks(sketch, far, corner, rows_each)
    def to_sender(i):
        return (i + stride if i % 2 == 0 else i - stride) % devices

    corners = [i for i in range(devices) if i % stride in (0, stride - 1)]
    corner = lax.ppermute(corner, AXES, [(i, to_sender(i)) for i in corners] + [(2, 4)])
    far_back = lax.ppermute(far_back, AXES, [(i, to_sender(i)) for i in range(devices)])
    sums = trade(sums, SECOND_GROUP)
    rows, token = pair_blocks(sketch, mate, near, far_block, far_back, corner, sums, rows)
    left, next_vector, stats, lost = finish(sums, basis, image, float(total_rows), token)

    m = basis.shape[0]

    def from_sums():
        return next_vector[0], stats[0, : m + 1]

    def from_vector():
        square = lax.psum(jnp.sum(left * left), AXES)
        beta = jnp.sqrt(square / total_rows + 1e-06)
        return left[0] / beta, jnp.concatenate([stats[0, :m], beta[None]])

    next_vector, coefficients = lax.cond(lost[0] != 0, from_vector, from_sums)
    return rows, next_vector, coefficients


def solution(mesh):
    grid = Mesh(np.asarray(mesh.devices).reshape(SIZES), AXES)
    return jax.shard_map(
        on_device,
        mesh=grid,
        in_specs=(P(AXES, None), P(None, AXES)),
        out_specs=(P(AXES, None), P(AXES), P()),
        check_vma=False,
    )
```

```python
import functools

import jax
import jax.numpy as jnp
import numpy as np
from jax import lax
from jax.experimental import pallas as pl
from jax.experimental.pallas import tpu as pltpu
from jax.sharding import Mesh
from jax.sharding import PartitionSpec as P

AXES = ("x", "z", "y", "core")
SIZES = (4, 8, 8, 2)
FIRST_GROUP = ("z", "core")
SECOND_GROUP = ("x", "y")
BANDS = 5
VMEM_BYTES = 16 * 1024 * 1024
LOAD_VMEM_BYTES = 16 * 1024 * 1024
EXTRA = 16
F32 = jnp.float32
BF16 = jnp.bfloat16


def dot_last(left, right, precision=None):
    return lax.dot_general(
        left, right, (((1,), (1,)), ((), ())), preferred_element_type=F32, precision=precision
    )


def params(**more):
    return pltpu.CompilerParams(vmem_limit_bytes=VMEM_BYTES, **more)


def whole(memory_space=pltpu.VMEM):
    return pl.BlockSpec(memory_space=memory_space)


def shaped(shape, dtype=F32):
    return jax.ShapeDtypeStruct(shape, dtype)


def load_kernel(chunks, sketch_hbm, basis_hbm, held_ref, u_ref, basis_ref, sems):
    last = basis_ref.shape[0] - 1
    rows, k = sketch_hbm.shape
    n = rows // chunks
    basis_copy = pltpu.make_async_copy(basis_hbm, basis_ref, sems.at[chunks])
    basis_copy.start()
    copies = []
    for i in range(chunks):
        piece = pl.ds(i * n, n)
        copies.append(pltpu.make_async_copy(sketch_hbm.at[piece], held_ref.at[piece], sems.at[i]))
        copies[i].start()
    basis_copy.wait()
    current = jnp.broadcast_to(basis_ref[last : last + 1, :], (EXTRA, rows))
    held_ref[rows:, :] = jnp.concatenate([current, jnp.zeros((EXTRA, k - rows), F32)], axis=1).astype(BF16)
    total = None
    for i in range(chunks):
        copies[i].wait()
        part = jnp.dot(
            current[:, i * n : (i + 1) * n].astype(BF16),
            held_ref[i * n : (i + 1) * n, :],
            preferred_element_type=F32,
        )
        total = part if total is None else total + part
    u_ref[...] = total[0:1, :]


def load_and_project(sketch, basis):
    chunks = 4
    n, k = sketch.shape
    return pl.pallas_call(
        functools.partial(load_kernel, chunks),
        out_shape=(shaped((n + EXTRA, k), BF16), shaped((1, k)), shaped(basis.shape)),
        in_specs=[whole(pltpu.HBM), whole(pltpu.HBM)],
        out_specs=(whole(), whole(), whole()),
        scratch_shapes=[pltpu.SemaphoreType.DMA((chunks + 1,))],
        compiler_params=pltpu.CompilerParams(vmem_limit_bytes=LOAD_VMEM_BYTES),
        cost_estimate=pl.CostEstimate(
            flops=2 * sketch.size, bytes_accessed=0, transcendentals=0
        ),
    )(sketch, basis)


def mate_kernel(mate_ref, u_ref):
    n = mate_ref.shape[0] - EXTRA
    product = jnp.dot(mate_ref[n:, :n], mate_ref[:n, :], preferred_element_type=F32)
    u_ref[...] = product[0:1, :]


def mate_projection(mate):
    return pl.pallas_call(
        mate_kernel,
        out_shape=shaped((1, mate.shape[1])),
        in_specs=[whole()],
        out_specs=whole(),
        compiler_params=params(),
        cost_estimate=pl.CostEstimate(flops=2 * mate.size, bytes_accessed=2 * mate.size, transcendentals=0),
    )(mate)


def column_copy(block_ref, rows_ref, column, sem):
    n = block_ref.shape[0]
    start = column * n if isinstance(column, int) else pl.multiple_of(column * n, n)
    return pltpu.make_async_copy(block_ref, rows_ref.at[:, pl.ds(start, n)], sem)


def plane_rank():
    rank, size = 0, 1
    for name in AXES[1:]:
        rank = rank * lax.axis_size(name) + lax.axis_index(name)
        size = size * lax.axis_size(name)
    return rank, size - 1


def own_blocks_kernel(sketch_ref, mate_ref, basis_ref, rows_ref, own_image_ref, mate_block_ref, block_ref, sem):
    last = basis_ref.shape[0] - 1
    n = block_ref.shape[0]
    current = basis_ref[last : last + 1, :].astype(BF16)
    sketch = sketch_ref[:n, :]
    block = dot_last(sketch, sketch).astype(BF16)
    block_ref[...] = block
    copy = column_copy(block_ref, rows_ref, 0, sem)
    copy.start()
    own_image_ref[...] = dot_last(jnp.broadcast_to(current, (16, n)), block)[0:1, :]
    mate_block_ref[...] = dot_last(sketch, mate_ref[:n, :]).astype(BF16)
    copy.wait()


def own_blocks(sketch, mate, basis):
    n, k = basis.shape[1], sketch.shape[1]
    return pl.pallas_call(
        own_blocks_kernel,
        out_shape=(shaped((n, BANDS * n), BF16), shaped((1, n)), shaped((n, n), BF16)),
        in_specs=[whole()] * 3,
        out_specs=(whole(pl.ANY), whole(), whole()),
        scratch_shapes=[pltpu.VMEM((n, n), BF16), pltpu.SemaphoreType.DMA],
        compiler_params=params(),
        cost_estimate=pl.CostEstimate(
            flops=4 * n * n * k, bytes_accessed=2 * n * k, transcendentals=0
        ),
    )(sketch, mate, basis)


def image_kernel(sketch_ref, basis_ref, own_ref, a_ref, b_ref, c_ref, d_ref, image_ref, sums_ref):
    rows = own_ref.shape[1]
    total = (a_ref[...] + b_ref[...]) + (c_ref[...] + d_ref[...])
    high = total.astype(BF16).astype(F32)
    rest = total - high
    middle = rest.astype(BF16).astype(F32)
    low = rest - middle
    row = lax.broadcasted_iota(jnp.int32, (16, total.shape[1]), 0)
    parts = jnp.where(row == 0, high, jnp.where(row == 1, middle, jnp.where(row == 2, low, 0.0)))
    product = dot_last(parts.astype(BF16), sketch_ref[:rows, :])
    image = (product[2:3, :] + product[1:2, :]) + product[0:1, :] + own_ref[...]
    image_ref[...] = image
    basis = basis_ref[...]
    m, n = basis.shape
    place = lax.broadcasted_iota(jnp.int32, (m, n), 0)
    right = jnp.concatenate([basis, jnp.where(place == 0, image, 0.0)] * m, axis=0)
    products = dot_last(basis, right, precision=lax.Precision.HIGHEST)
    norm = jnp.sum(image * image)
    lane = lax.broadcasted_iota(jnp.int32, products.shape, 1)
    line = lax.broadcasted_iota(jnp.int32, products.shape, 0)
    kept = jnp.where((lane // (2 * m)) == line, products, 0.0)
    packed = jnp.sum(kept, axis=0, keepdims=True)
    packed = jnp.where(lane[0:1, :] == m + 1, norm, packed)
    sums_ref[...] = jnp.broadcast_to(packed, sums_ref.shape)


def image_and_sums(sketch, basis, own_image, parts, copies):
    n, k = basis.shape[1], sketch.shape[1]
    return pl.pallas_call(
        image_kernel,
        out_shape=(shaped((1, n)), shaped((copies, 16 * basis.shape[0]))),
        in_specs=[whole()] * 7,
        out_specs=(whole(), whole()),
        compiler_params=params(),
        cost_estimate=pl.CostEstimate(
            flops=2 * n * k * 16, bytes_accessed=2 * n * k, transcendentals=0
        ),
    )(sketch, basis, own_image, *parts)


def add_kernel(rows_ref, copies_ref):
    total = jnp.sum(rows_ref[...], axis=0, keepdims=True)
    copies_ref[...] = jnp.broadcast_to(total, copies_ref.shape)


def add_and_copy(rows, copies):
    return pl.pallas_call(
        add_kernel,
        out_shape=shaped((copies, rows.shape[1])),
        in_specs=[whole()],
        out_specs=whole(),
        compiler_params=params(),
    )(rows)


def near_kernel(
    sketch_ref, far_ref, near_ref, mate_block_ref, token_ref, rows_in_ref, rows_ref, block_ref, sem
):
    del token_ref, rows_in_ref
    copy = column_copy(mate_block_ref, rows_ref, 1 + lax.axis_index("core"), sem)
    copy.start()
    rank, last = plane_rank()
    is_corner = (rank == 0) | (rank == last)

    @pl.when(is_corner)
    def _():
        block_ref[...] = dot_last(far_ref[...], near_ref[...]).astype(BF16)

    @pl.when(jnp.logical_not(is_corner))
    def _():
        block_ref[...] = dot_last(sketch_ref[: block_ref.shape[0], :], near_ref[...]).astype(BF16)

    copy.wait()


def near_block(sketch, far, near, mate_block, token, rows):
    n, k = near.shape
    return pl.pallas_call(
        near_kernel,
        out_shape=(shaped(rows.shape, rows.dtype), shaped((n, n), BF16)),
        in_specs=[whole()] * 5 + [whole(pl.ANY)],
        out_specs=(whole(pl.ANY), whole()),
        scratch_shapes=[pltpu.SemaphoreType.DMA],
        input_output_aliases={5: 0},
        compiler_params=params(),
        cost_estimate=pl.CostEstimate(
            flops=2 * n * n * k, bytes_accessed=4 * n * k, transcendentals=0
        ),
    )(sketch, far, near, mate_block, token, rows)


def far_kernel(sketch_ref, far_ref, near_block_ref, rows_in_ref, rows_ref, back_ref, block_ref, sem):
    del rows_in_ref
    copy = column_copy(near_block_ref, rows_ref, 2 - lax.axis_index("core"), sem)
    copy.start()
    back = dot_last(far_ref[...], sketch_ref[: back_ref.shape[0], :]).astype(BF16)
    back_ref[...] = back
    block_ref[...] = back.T
    copy.wait()


def far_blocks(sketch, far, near_block, rows):
    n, k = far.shape
    block = shaped((n, n), BF16)
    return pl.pallas_call(
        far_kernel,
        out_shape=(shaped(rows.shape, rows.dtype), block, block),
        in_specs=[whole()] * 3 + [whole(pl.ANY)],
        out_specs=(whole(pl.ANY), whole(), whole()),
        scratch_shapes=[pltpu.SemaphoreType.DMA],
        input_output_aliases={3: 0},
        compiler_params=params(),
        cost_estimate=pl.CostEstimate(
            flops=2 * n * n * k, bytes_accessed=4 * n * k, transcendentals=0
        ),
    )(sketch, far, near_block, rows)


def place_corner_kernel(corner_ref, rows_in_ref, rows_ref, sem):
    del rows_in_ref
    rank, last = plane_rank()

    @pl.when((rank == 0) | (rank == last))
    def _():
        copy = column_copy(corner_ref, rows_ref, 2 - lax.axis_index("core"), sem)
        copy.start()
        copy.wait()


def place_corner(corner, rows):
    return pl.pallas_call(
        place_corner_kernel,
        out_shape=shaped(rows.shape, rows.dtype),
        in_specs=[whole(), whole(pl.ANY)],
        out_specs=whole(pl.ANY),
        scratch_shapes=[pltpu.SemaphoreType.DMA],
        input_output_aliases={1: 0},
        compiler_params=params(),
        cost_estimate=pl.CostEstimate(flops=0, bytes_accessed=2 * corner.size, transcendentals=0),
    )(corner, rows)


def place_far_kernel(far_ref, back_ref, rows_in_ref, rows_ref, token_ref, sems):
    del rows_in_ref
    token_ref[...] = jnp.zeros_like(token_ref)
    core = lax.axis_index("core")
    far = column_copy(far_ref, rows_ref, 3 + core, sems.at[0])
    back = column_copy(back_ref, rows_ref, 4 - core, sems.at[1])
    far.start()
    back.start()
    far.wait()
    back.wait()


def place_far(far, back, rows):
    return pl.pallas_call(
        place_far_kernel,
        out_shape=(shaped(rows.shape, rows.dtype), shaped((8, 128))),
        in_specs=[whole()] * 2 + [whole(pl.ANY)],
        out_specs=(whole(pl.ANY), whole()),
        scratch_shapes=[pltpu.SemaphoreType.DMA((2,))],
        input_output_aliases={2: 0},
        compiler_params=params(),
        cost_estimate=pl.CostEstimate(flops=0, bytes_accessed=8 * far.size, transcendentals=0),
    )(far, back, rows)


def finish_kernel(count, sums_ref, basis_ref, image_ref, token_ref, left_ref, next_ref, stats_ref, lost_ref):
    del token_ref
    sums = jnp.sum(sums_ref[...], axis=0, keepdims=True)
    basis = basis_ref[...]
    m = basis.shape[0]
    shape = (m, sums.shape[1])
    line = lax.broadcasted_iota(jnp.int32, shape, 0)
    lane = lax.broadcasted_iota(jnp.int32, shape, 1)
    major, minor = lane // (2 * m), lane % (2 * m)
    spread = jnp.broadcast_to(sums, shape)
    inner = jnp.sum(jnp.where((major == line) & (minor == m), spread, 0.0), axis=1, keepdims=True)
    norm = jnp.sum(jnp.where(lane[0:1, :] == m + 1, sums, 0.0), axis=1, keepdims=True)
    coeffs = inner / count
    by_major = jnp.sum(jnp.where(major == line, coeffs, 0.0), axis=0, keepdims=True)
    by_minor = jnp.sum(jnp.where(minor == line, coeffs, 0.0), axis=0, keepdims=True)
    by_lane = jnp.sum(jnp.where(lane == line, coeffs, 0.0), axis=0, keepdims=True)
    quadratic = jnp.sum(sums * by_major * by_minor, axis=1, keepdims=True)
    cross = jnp.sum(coeffs * inner, axis=0, keepdims=True)
    square = (norm - cross) + (quadratic - cross)
    beta = jnp.sqrt(jnp.maximum(square, 0.0) / count + 1e-06)
    left = image_ref[...] - jnp.sum(coeffs * basis, axis=0, keepdims=True)
    left_ref[...] = left
    next_ref[...] = left / beta
    stats_ref[...] = jnp.where(lane[0:1, :] == m, beta, by_lane)
    largest = norm + cross + jnp.abs(quadratic)
    lost_ref[0] = jnp.max(jnp.where(square < 1e-3 * largest, 1.0, 0.0)).astype(jnp.int32)


def finish(sums, basis, image, count, token):
    row = shaped(image.shape)
    return pl.pallas_call(
        functools.partial(finish_kernel, count),
        out_shape=(row, row, shaped((1, 128)), shaped((1,), jnp.int32)),
        in_specs=[whole()] * 4,
        out_specs=(whole(), whole(), whole(), whole(pltpu.SMEM)),
        compiler_params=params(),
    )(sums, basis, image, token)


def group_size(group):
    members = 1
    for name in group:
        members *= lax.axis_size(name)
    return members


def on_device(sketch, basis):
    devices = group_size(AXES)
    stride = devices // SIZES[0]
    total_rows = basis.shape[1] * devices

    def move(block, source_of):
        return lax.ppermute(block, AXES, [(source_of(i) % devices, i) for i in range(devices)])

    def trade(rows, group):
        return lax.all_to_all(rows, group, 0, 0, tiled=True)

    def in_plane(i, step):
        return i // stride * stride + (i + step) % stride

    far = move(sketch, lambda i: i + stride if i % 2 == 0 else i - stride)
    near = move(sketch, lambda i: in_plane(i, -1 if i % 2 == 0 else 1))
    stored = [pltpu.with_memory_space_constraint(array, pltpu.HBM) for array in (sketch, basis)]
    sketch, u, basis = load_and_project(*stored)
    mate = move(sketch, lambda i: i ^ 1)
    mate_u = mate_projection(mate)
    parts = (
        move(u, lambda i: i - stride if i % 2 == 0 else i + stride),
        move(mate_u, lambda i: i + stride + 1 if i % 2 == 0 else i - stride - 1),
        move(mate_u, lambda i: i - 2 if i % 2 == 0 else i + 2),
        mate_u,
    )
    rows, own_image, mate_block = own_blocks(sketch, mate, basis)
    image, sums = image_and_sums(sketch, basis, own_image, parts, group_size(FIRST_GROUP))
    sums = add_and_copy(trade(sums, FIRST_GROUP), group_size(SECOND_GROUP))
    rows, near = near_block(sketch, far, near, mate_block, sums, rows)
    rows, far_back, far_block = far_blocks(sketch, far, near, rows)
    def to_sender(i):
        return (i + stride if i % 2 == 0 else i - stride) % devices

    corners = [i for i in range(devices) if i % stride in (0, stride - 1)]
    corner = lax.ppermute(near, AXES, [(i, to_sender(i)) for i in corners] + [(2, 4)])
    far_back = lax.ppermute(far_back, AXES, [(i, to_sender(i)) for i in range(devices)])
    sums = trade(sums, SECOND_GROUP)
    rows = place_corner(corner, rows)
    rows, token = place_far(far_block, far_back, rows)
    left, next_vector, stats, lost = finish(sums, basis, image, float(total_rows), token)

    m = basis.shape[0]

    def from_sums():
        return next_vector[0], stats[0, : m + 1]

    def from_vector():
        square = lax.psum(jnp.sum(left * left), AXES)
        beta = jnp.sqrt(square / total_rows + 1e-06)
        return left[0] / beta, jnp.concatenate([stats[0, :m], beta[None]])

    next_vector, coefficients = lax.cond(lost[0] != 0, from_vector, from_sums)
    return rows, next_vector, coefficients


def solution(mesh):
    grid = Mesh(np.asarray(mesh.devices).reshape(SIZES), AXES)
    return jax.shard_map(
        on_device,
        mesh=grid,
        in_specs=(P(AXES, None), P(None, AXES)),
        out_specs=(P(AXES, None), P(AXES), P()),
        check_vma=False,
    )
```

```python
import functools

import jax
import jax.numpy as jnp
import numpy as np
from jax import lax
from jax.experimental import pallas as pl
from jax.experimental.pallas import tpu as pltpu
from jax.sharding import Mesh
from jax.sharding import PartitionSpec as P

AXES = ("x", "z", "y", "core")
SIZES = (4, 8, 8, 2)
FIRST_GROUP = ("z", "core")
SECOND_GROUP = ("x", "y")
BANDS = 5
VMEM_BYTES = 16 * 1024 * 1024
LOAD_VMEM_BYTES = 16 * 1024 * 1024
EXTRA = 16
F32 = jnp.float32
BF16 = jnp.bfloat16


def dot_last(left, right, precision=None):
    return lax.dot_general(
        left, right, (((1,), (1,)), ((), ())), preferred_element_type=F32, precision=precision
    )


def params(**more):
    return pltpu.CompilerParams(vmem_limit_bytes=VMEM_BYTES, **more)


def whole(memory_space=pltpu.VMEM):
    return pl.BlockSpec(memory_space=memory_space)


def shaped(shape, dtype=F32):
    return jax.ShapeDtypeStruct(shape, dtype)


def load_kernel(chunks, sketch_hbm, basis_hbm, held_ref, u_ref, basis_ref, sems):
    last = basis_ref.shape[0] - 1
    rows, k = sketch_hbm.shape
    n = rows // chunks
    basis_copy = pltpu.make_async_copy(basis_hbm, basis_ref, sems.at[chunks])
    basis_copy.start()
    copies = []
    for i in range(chunks):
        piece = pl.ds(i * n, n)
        copies.append(pltpu.make_async_copy(sketch_hbm.at[piece], held_ref.at[piece], sems.at[i]))
        copies[i].start()
    basis_copy.wait()
    current = jnp.broadcast_to(basis_ref[last : last + 1, :], (EXTRA, rows))
    held_ref[rows:, :] = jnp.concatenate([current, jnp.zeros((EXTRA, k - rows), F32)], axis=1).astype(BF16)
    total = None
    for i in range(chunks):
        copies[i].wait()
        part = jnp.dot(
            current[:, i * n : (i + 1) * n].astype(BF16),
            held_ref[i * n : (i + 1) * n, :],
            preferred_element_type=F32,
        )
        total = part if total is None else total + part
    u_ref[...] = total[0:1, :]


def load_and_project(sketch, basis):
    chunks = 4
    n, k = sketch.shape
    return pl.pallas_call(
        functools.partial(load_kernel, chunks),
        out_shape=(shaped((n + EXTRA, k), BF16), shaped((1, k)), shaped(basis.shape)),
        in_specs=[whole(pltpu.HBM), whole(pltpu.HBM)],
        out_specs=(whole(), whole(), whole()),
        scratch_shapes=[pltpu.SemaphoreType.DMA((chunks + 1,))],
        compiler_params=pltpu.CompilerParams(vmem_limit_bytes=LOAD_VMEM_BYTES),
        cost_estimate=pl.CostEstimate(
            flops=2 * sketch.size, bytes_accessed=0, transcendentals=0
        ),
    )(sketch, basis)


def mate_kernel(mate_ref, own_u_ref, mate_u_ref, both_ref):
    n = mate_ref.shape[0] - EXTRA
    product = jnp.dot(mate_ref[n:, :n], mate_ref[:n, :], preferred_element_type=F32)
    mate_u = product[0:1, :]
    mate_u_ref[...] = mate_u
    is_first = lax.axis_index("core") == 0
    both_ref[0:1, :] = jnp.where(is_first, own_u_ref[...], mate_u)
    both_ref[1:2, :] = jnp.where(is_first, mate_u, own_u_ref[...])


def mate_projection(mate, u):
    return pl.pallas_call(
        mate_kernel,
        out_shape=(shaped((1, mate.shape[1])), shaped((2, mate.shape[1]))),
        in_specs=[whole(), whole()],
        out_specs=(whole(), whole()),
        compiler_params=params(),
        cost_estimate=pl.CostEstimate(flops=2 * mate.size, bytes_accessed=2 * mate.size, transcendentals=0),
    )(mate, u)


def column_copy(block_ref, rows_ref, column, sem):
    n = block_ref.shape[0]
    start = column * n if isinstance(column, int) else pl.multiple_of(column * n, n)
    return pltpu.make_async_copy(block_ref, rows_ref.at[:, pl.ds(start, n)], sem)


def plane_rank():
    rank, size = 0, 1
    for name in AXES[1:]:
        rank = rank * lax.axis_size(name) + lax.axis_index(name)
        size = size * lax.axis_size(name)
    return rank, size - 1


def own_blocks_kernel(sketch_ref, mate_ref, basis_ref, rows_ref, own_image_ref, mate_block_ref, block_ref, sem):
    last = basis_ref.shape[0] - 1
    n = block_ref.shape[0]
    current = basis_ref[last : last + 1, :].astype(BF16)
    sketch = sketch_ref[:n, :]
    block = dot_last(sketch, sketch).astype(BF16)
    block_ref[...] = block
    copy = column_copy(block_ref, rows_ref, 0, sem)
    copy.start()
    own_image_ref[...] = dot_last(jnp.broadcast_to(current, (16, n)), block)[0:1, :]
    mate_block_ref[...] = dot_last(sketch, mate_ref[:n, :]).astype(BF16)
    copy.wait()


def own_blocks(sketch, mate, basis):
    n, k = basis.shape[1], sketch.shape[1]
    return pl.pallas_call(
        own_blocks_kernel,
        out_shape=(shaped((n, BANDS * n), BF16), shaped((1, n)), shaped((n, n), BF16)),
        in_specs=[whole()] * 3,
        out_specs=(whole(pl.ANY), whole(), whole()),
        scratch_shapes=[pltpu.VMEM((n, n), BF16), pltpu.SemaphoreType.DMA],
        compiler_params=params(),
        cost_estimate=pl.CostEstimate(
            flops=4 * n * n * k, bytes_accessed=2 * n * k, transcendentals=0
        ),
    )(sketch, mate, basis)


def image_kernel(sketch_ref, basis_ref, own_ref, a_ref, b_ref, c_ref, d_ref, image_ref, sums_ref):
    rows = own_ref.shape[1]
    far = a_ref[...] + b_ref[...]
    far = jnp.where(lax.axis_index("core") == 0, far[0:1, :], far[1:2, :])
    total = far + (c_ref[...] + d_ref[...])
    high = total.astype(BF16).astype(F32)
    rest = total - high
    middle = rest.astype(BF16).astype(F32)
    low = rest - middle
    row = lax.broadcasted_iota(jnp.int32, (16, total.shape[1]), 0)
    parts = jnp.where(row == 0, high, jnp.where(row == 1, middle, jnp.where(row == 2, low, 0.0)))
    product = dot_last(parts.astype(BF16), sketch_ref[:rows, :])
    image = (product[2:3, :] + product[1:2, :]) + product[0:1, :] + own_ref[...]
    image_ref[...] = image
    basis = basis_ref[...]
    m, n = basis.shape
    place = lax.broadcasted_iota(jnp.int32, (m, n), 0)
    right = jnp.concatenate([basis, jnp.where(place == 0, image, 0.0)] * m, axis=0)
    products = dot_last(basis, right, precision=lax.Precision.HIGHEST)
    norm = jnp.sum(image * image)
    lane = lax.broadcasted_iota(jnp.int32, products.shape, 1)
    line = lax.broadcasted_iota(jnp.int32, products.shape, 0)
    kept = jnp.where((lane // (2 * m)) == line, products, 0.0)
    packed = jnp.sum(kept, axis=0, keepdims=True)
    packed = jnp.where(lane[0:1, :] == m + 1, norm, packed)
    sums_ref[...] = jnp.broadcast_to(packed, sums_ref.shape)


def image_and_sums(sketch, basis, own_image, parts, copies):
    n, k = basis.shape[1], sketch.shape[1]
    return pl.pallas_call(
        image_kernel,
        out_shape=(shaped((1, n)), shaped((copies, 16 * basis.shape[0]))),
        in_specs=[whole()] * 7,
        out_specs=(whole(), whole()),
        compiler_params=params(),
        cost_estimate=pl.CostEstimate(
            flops=2 * n * k * 16, bytes_accessed=2 * n * k, transcendentals=0
        ),
    )(sketch, basis, own_image, *parts)


def add_kernel(rows_ref, copies_ref):
    total = jnp.sum(rows_ref[...], axis=0, keepdims=True)
    copies_ref[...] = jnp.broadcast_to(total, copies_ref.shape)


def add_and_copy(rows, copies):
    return pl.pallas_call(
        add_kernel,
        out_shape=shaped((copies, rows.shape[1])),
        in_specs=[whole()],
        out_specs=whole(),
        compiler_params=params(),
    )(rows)


def near_kernel(
    sketch_ref, far_ref, near_ref, mate_block_ref, token_ref, rows_in_ref, rows_ref, block_ref, sem
):
    del token_ref, rows_in_ref
    copy = column_copy(mate_block_ref, rows_ref, 1 + lax.axis_index("core"), sem)
    copy.start()
    rank, last = plane_rank()
    is_corner = (rank == 0) | (rank == last)

    @pl.when(is_corner)
    def _():
        block_ref[...] = dot_last(far_ref[...], near_ref[...]).astype(BF16)

    @pl.when(jnp.logical_not(is_corner))
    def _():
        block_ref[...] = dot_last(sketch_ref[: block_ref.shape[0], :], near_ref[...]).astype(BF16)

    copy.wait()


def near_block(sketch, far, near, mate_block, token, rows):
    n, k = near.shape
    return pl.pallas_call(
        near_kernel,
        out_shape=(shaped(rows.shape, rows.dtype), shaped((n, n), BF16)),
        in_specs=[whole()] * 5 + [whole(pl.ANY)],
        out_specs=(whole(pl.ANY), whole()),
        scratch_shapes=[pltpu.SemaphoreType.DMA],
        input_output_aliases={5: 0},
        compiler_params=params(),
        cost_estimate=pl.CostEstimate(
            flops=2 * n * n * k, bytes_accessed=4 * n * k, transcendentals=0
        ),
    )(sketch, far, near, mate_block, token, rows)


def far_kernel(sketch_ref, far_ref, near_block_ref, rows_in_ref, rows_ref, back_ref, block_ref, sem):
    del rows_in_ref
    copy = column_copy(near_block_ref, rows_ref, 2 - lax.axis_index("core"), sem)
    copy.start()
    back = dot_last(far_ref[...], sketch_ref[: back_ref.shape[0], :]).astype(BF16)
    back_ref[...] = back
    block_ref[...] = back.T
    copy.wait()


def far_blocks(sketch, far, near_block, rows):
    n, k = far.shape
    block = shaped((n, n), BF16)
    return pl.pallas_call(
        far_kernel,
        out_shape=(shaped(rows.shape, rows.dtype), block, block),
        in_specs=[whole()] * 3 + [whole(pl.ANY)],
        out_specs=(whole(pl.ANY), whole(), whole()),
        scratch_shapes=[pltpu.SemaphoreType.DMA],
        input_output_aliases={3: 0},
        compiler_params=params(),
        cost_estimate=pl.CostEstimate(
            flops=2 * n * n * k, bytes_accessed=4 * n * k, transcendentals=0
        ),
    )(sketch, far, near_block, rows)


def place_corner_kernel(corner_ref, rows_in_ref, rows_ref, sem):
    del rows_in_ref
    rank, last = plane_rank()

    @pl.when((rank == 0) | (rank == last))
    def _():
        copy = column_copy(corner_ref, rows_ref, 2 - lax.axis_index("core"), sem)
        copy.start()
        copy.wait()


def place_corner(corner, rows):
    return pl.pallas_call(
        place_corner_kernel,
        out_shape=shaped(rows.shape, rows.dtype),
        in_specs=[whole(), whole(pl.ANY)],
        out_specs=whole(pl.ANY),
        scratch_shapes=[pltpu.SemaphoreType.DMA],
        input_output_aliases={1: 0},
        compiler_params=params(),
        cost_estimate=pl.CostEstimate(flops=0, bytes_accessed=2 * corner.size, transcendentals=0),
    )(corner, rows)


def place_far_kernel(far_ref, back_ref, rows_in_ref, rows_ref, token_ref, sems):
    del rows_in_ref
    token_ref[...] = jnp.zeros_like(token_ref)
    core = lax.axis_index("core")
    far = column_copy(far_ref, rows_ref, 3 + core, sems.at[0])
    back = column_copy(back_ref, rows_ref, 4 - core, sems.at[1])
    far.start()
    back.start()
    far.wait()
    back.wait()


def place_far(far, back, rows):
    return pl.pallas_call(
        place_far_kernel,
        out_shape=(shaped(rows.shape, rows.dtype), shaped((8, 128))),
        in_specs=[whole()] * 2 + [whole(pl.ANY)],
        out_specs=(whole(pl.ANY), whole()),
        scratch_shapes=[pltpu.SemaphoreType.DMA((2,))],
        input_output_aliases={2: 0},
        compiler_params=params(),
        cost_estimate=pl.CostEstimate(flops=0, bytes_accessed=8 * far.size, transcendentals=0),
    )(far, back, rows)


def finish_kernel(count, sums_ref, basis_ref, image_ref, token_ref, left_ref, next_ref, stats_ref, lost_ref):
    del token_ref
    sums = jnp.sum(sums_ref[...], axis=0, keepdims=True)
    basis = basis_ref[...]
    m = basis.shape[0]
    shape = (m, sums.shape[1])
    line = lax.broadcasted_iota(jnp.int32, shape, 0)
    lane = lax.broadcasted_iota(jnp.int32, shape, 1)
    major, minor = lane // (2 * m), lane % (2 * m)
    spread = jnp.broadcast_to(sums, shape)
    inner = jnp.sum(jnp.where((major == line) & (minor == m), spread, 0.0), axis=1, keepdims=True)
    norm = jnp.sum(jnp.where(lane[0:1, :] == m + 1, sums, 0.0), axis=1, keepdims=True)
    coeffs = inner / count
    by_major = jnp.sum(jnp.where(major == line, coeffs, 0.0), axis=0, keepdims=True)
    by_minor = jnp.sum(jnp.where(minor == line, coeffs, 0.0), axis=0, keepdims=True)
    by_lane = jnp.sum(jnp.where(lane == line, coeffs, 0.0), axis=0, keepdims=True)
    quadratic = jnp.sum(sums * by_major * by_minor, axis=1, keepdims=True)
    cross = jnp.sum(coeffs * inner, axis=0, keepdims=True)
    square = (norm - cross) + (quadratic - cross)
    beta = jnp.sqrt(jnp.maximum(square, 0.0) / count + 1e-06)
    left = image_ref[...] - jnp.sum(coeffs * basis, axis=0, keepdims=True)
    left_ref[...] = left
    next_ref[...] = left / beta
    stats_ref[...] = jnp.where(lane[0:1, :] == m, beta, by_lane)
    largest = norm + cross + jnp.abs(quadratic)
    lost_ref[0] = jnp.max(jnp.where(square < 1e-3 * largest, 1.0, 0.0)).astype(jnp.int32)


def finish(sums, basis, image, count, token):
    row = shaped(image.shape)
    return pl.pallas_call(
        functools.partial(finish_kernel, count),
        out_shape=(row, row, shaped((1, 128)), shaped((1,), jnp.int32)),
        in_specs=[whole()] * 4,
        out_specs=(whole(), whole(), whole(), whole(pltpu.SMEM)),
        compiler_params=params(),
    )(sums, basis, image, token)


def group_size(group):
    members = 1
    for name in group:
        members *= lax.axis_size(name)
    return members


def on_device(sketch, basis):
    devices = group_size(AXES)
    stride = devices // SIZES[0]
    total_rows = basis.shape[1] * devices

    def move(block, source_of):
        return lax.ppermute(block, AXES, [(source_of(i) % devices, i) for i in range(devices)])

    def trade(rows, group):
        return lax.all_to_all(rows, group, 0, 0, tiled=True)

    def in_plane(i, step):
        return i // stride * stride + (i + step) % stride

    far = move(sketch, lambda i: i + stride if i % 2 == 0 else i - stride)
    near = move(sketch, lambda i: in_plane(i, -1 if i % 2 == 0 else 1))
    stored = [pltpu.with_memory_space_constraint(array, pltpu.HBM) for array in (sketch, basis)]
    sketch, u, basis = load_and_project(*stored)
    mate = move(sketch, lambda i: i ^ 1)
    mate_u, both_u = mate_projection(mate, u)
    far_u = move(both_u, lambda i: i - stride if i % 2 == 0 else i + stride)
    parts = (
        far_u,
        move(far_u, lambda i: i ^ 1),
        move(mate_u, lambda i: i - 2 if i % 2 == 0 else i + 2),
        mate_u,
    )
    rows, own_image, mate_block = own_blocks(sketch, mate, basis)
    image, sums = image_and_sums(sketch, basis, own_image, parts, group_size(FIRST_GROUP))
    sums = add_and_copy(trade(sums, FIRST_GROUP), group_size(SECOND_GROUP))
    rows, near = near_block(sketch, far, near, mate_block, sums, rows)
    rows, far_back, far_block = far_blocks(sketch, far, near, rows)
    def to_sender(i):
        return (i + stride if i % 2 == 0 else i - stride) % devices

    corners = [i for i in range(devices) if i % stride in (0, stride - 1)]
    corner = lax.ppermute(near, AXES, [(i, to_sender(i)) for i in corners] + [(2, 4)])
    far_back = lax.ppermute(far_back, AXES, [(i, to_sender(i)) for i in range(devices)])
    sums = trade(sums, SECOND_GROUP)
    rows = place_corner(corner, rows)
    rows, token = place_far(far_block, far_back, rows)
    left, next_vector, stats, lost = finish(sums, basis, image, float(total_rows), token)

    m = basis.shape[0]

    def from_sums():
        return next_vector[0], stats[0, : m + 1]

    def from_vector():
        square = lax.psum(jnp.sum(left * left), AXES)
        beta = jnp.sqrt(square / total_rows + 1e-06)
        return left[0] / beta, jnp.concatenate([stats[0, :m], beta[None]])

    next_vector, coefficients = lax.cond(lost[0] != 0, from_vector, from_sums)
    return rows, next_vector, coefficients


def solution(mesh):
    grid = Mesh(np.asarray(mesh.devices).reshape(SIZES), AXES)
    return jax.shard_map(
        on_device,
        mesh=grid,
        in_specs=(P(AXES, None), P(None, AXES)),
        out_specs=(P(AXES, None), P(AXES), P()),
        check_vma=False,
    )
```

```python
import functools

import jax
import jax.numpy as jnp
import numpy as np
from jax import lax
from jax.experimental import pallas as pl
from jax.experimental.pallas import tpu as pltpu
from jax.sharding import Mesh
from jax.sharding import PartitionSpec as P

AXES = ("x", "z", "y", "core")
SIZES = (4, 8, 8, 2)
FIRST_GROUP = ("z", "core")
SECOND_GROUP = ("x", "y")
BANDS = 5
VMEM_BYTES = 16 * 1024 * 1024
LOAD_VMEM_BYTES = 16 * 1024 * 1024
EXTRA = 16
F32 = jnp.float32
BF16 = jnp.bfloat16


def dot_last(left, right, precision=None):
    return lax.dot_general(
        left, right, (((1,), (1,)), ((), ())), preferred_element_type=F32, precision=precision
    )


def params(**more):
    return pltpu.CompilerParams(vmem_limit_bytes=VMEM_BYTES, **more)


def whole(memory_space=pltpu.VMEM):
    return pl.BlockSpec(memory_space=memory_space)


def shaped(shape, dtype=F32):
    return jax.ShapeDtypeStruct(shape, dtype)


def load_kernel(chunks, sketch_hbm, basis_hbm, held_ref, u_ref, basis_ref, sems):
    last = basis_ref.shape[0] - 1
    rows, k = sketch_hbm.shape
    n = rows // chunks
    basis_copy = pltpu.make_async_copy(basis_hbm, basis_ref, sems.at[chunks])
    basis_copy.start()
    copies = []
    for i in range(chunks):
        piece = pl.ds(i * n, n)
        copies.append(pltpu.make_async_copy(sketch_hbm.at[piece], held_ref.at[piece], sems.at[i]))
        copies[i].start()
    basis_copy.wait()
    current = jnp.broadcast_to(basis_ref[last : last + 1, :], (EXTRA, rows))
    held_ref[rows:, :] = jnp.concatenate([current, jnp.zeros((EXTRA, k - rows), F32)], axis=1).astype(BF16)
    total = None
    for i in range(chunks):
        copies[i].wait()
        part = jnp.dot(
            current[:, i * n : (i + 1) * n].astype(BF16),
            held_ref[i * n : (i + 1) * n, :],
            preferred_element_type=F32,
        )
        total = part if total is None else total + part
    u_ref[...] = total[0:1, :]


def load_and_project(sketch, basis):
    chunks = 4
    n, k = sketch.shape
    return pl.pallas_call(
        functools.partial(load_kernel, chunks),
        out_shape=(shaped((n + EXTRA, k), BF16), shaped((1, k)), shaped(basis.shape)),
        in_specs=[whole(pltpu.HBM), whole(pltpu.HBM)],
        out_specs=(whole(), whole(), whole()),
        scratch_shapes=[pltpu.SemaphoreType.DMA((chunks + 1,))],
        compiler_params=pltpu.CompilerParams(vmem_limit_bytes=LOAD_VMEM_BYTES),
        cost_estimate=pl.CostEstimate(
            flops=2 * sketch.size, bytes_accessed=0, transcendentals=0
        ),
    )(sketch, basis)


def mate_kernel(mate_ref, own_u_ref, mate_u_ref, both_ref):
    n = mate_ref.shape[0] - EXTRA
    product = jnp.dot(mate_ref[n:, :n], mate_ref[:n, :], preferred_element_type=F32)
    mate_u = product[0:1, :]
    mate_u_ref[...] = mate_u
    is_first = lax.axis_index("core") == 0
    both_ref[0:1, :] = jnp.where(is_first, own_u_ref[...], mate_u)
    both_ref[1:2, :] = jnp.where(is_first, mate_u, own_u_ref[...])


def mate_projection(mate, u):
    return pl.pallas_call(
        mate_kernel,
        out_shape=(shaped((1, mate.shape[1])), shaped((2, mate.shape[1]))),
        in_specs=[whole(), whole()],
        out_specs=(whole(), whole()),
        compiler_params=params(),
        cost_estimate=pl.CostEstimate(flops=2 * mate.size, bytes_accessed=2 * mate.size, transcendentals=0),
    )(mate, u)


def column_copy(block_ref, rows_ref, column, sem):
    n = block_ref.shape[0]
    start = column * n if isinstance(column, int) else pl.multiple_of(column * n, n)
    return pltpu.make_async_copy(block_ref, rows_ref.at[:, pl.ds(start, n)], sem)


def plane_rank():
    rank, size = 0, 1
    for name in AXES[1:]:
        rank = rank * lax.axis_size(name) + lax.axis_index(name)
        size = size * lax.axis_size(name)
    return rank, size - 1


def own_blocks_kernel(sketch_ref, mate_ref, basis_ref, rows_ref, own_image_ref, mate_block_ref, block_ref, sem):
    last = basis_ref.shape[0] - 1
    n = block_ref.shape[0]
    current = basis_ref[last : last + 1, :].astype(BF16)
    sketch = sketch_ref[:n, :]
    block = dot_last(sketch, sketch).astype(BF16)
    block_ref[...] = block
    copy = column_copy(block_ref, rows_ref, 0, sem)
    copy.start()
    own_image_ref[...] = dot_last(jnp.broadcast_to(current, (16, n)), block)[0:1, :]
    mate_block_ref[...] = dot_last(sketch, mate_ref[:n, :]).astype(BF16)
    copy.wait()


def own_blocks(sketch, mate, basis):
    n, k = basis.shape[1], sketch.shape[1]
    return pl.pallas_call(
        own_blocks_kernel,
        out_shape=(shaped((n, BANDS * n), BF16), shaped((1, n)), shaped((n, n), BF16)),
        in_specs=[whole()] * 3,
        out_specs=(whole(pl.ANY), whole(), whole()),
        scratch_shapes=[pltpu.VMEM((n, n), BF16), pltpu.SemaphoreType.DMA],
        compiler_params=params(),
        cost_estimate=pl.CostEstimate(
            flops=4 * n * n * k, bytes_accessed=2 * n * k, transcendentals=0
        ),
    )(sketch, mate, basis)


def image_kernel(sketch_ref, basis_ref, own_ref, a_ref, b_ref, c_ref, d_ref, image_ref, sums_ref):
    rows = own_ref.shape[1]
    far = a_ref[...] + b_ref[...]
    far = jnp.where(lax.axis_index("core") == 0, far[0:1, :], far[1:2, :])
    total = far + (c_ref[...] + d_ref[...])
    high = total.astype(BF16).astype(F32)
    rest = total - high
    middle = rest.astype(BF16).astype(F32)
    low = rest - middle
    row = lax.broadcasted_iota(jnp.int32, (16, total.shape[1]), 0)
    parts = jnp.where(row == 0, high, jnp.where(row == 1, middle, jnp.where(row == 2, low, 0.0)))
    product = dot_last(parts.astype(BF16), sketch_ref[:rows, :])
    image = (product[2:3, :] + product[1:2, :]) + product[0:1, :] + own_ref[...]
    image_ref[...] = image
    basis = basis_ref[...]
    m, n = basis.shape
    place = lax.broadcasted_iota(jnp.int32, (m, n), 0)
    right = jnp.concatenate([basis, jnp.where(place == 0, image, 0.0)] * m, axis=0)
    products = dot_last(basis, right, precision=lax.Precision.HIGHEST)
    norm = jnp.sum(image * image)
    lane = lax.broadcasted_iota(jnp.int32, products.shape, 1)
    line = lax.broadcasted_iota(jnp.int32, products.shape, 0)
    kept = jnp.where((lane // (2 * m)) == line, products, 0.0)
    packed = jnp.sum(kept, axis=0, keepdims=True)
    packed = jnp.where(lane[0:1, :] == m + 1, norm, packed)
    sums_ref[...] = jnp.broadcast_to(packed, sums_ref.shape)


def image_and_sums(sketch, basis, own_image, parts, copies):
    n, k = basis.shape[1], sketch.shape[1]
    return pl.pallas_call(
        image_kernel,
        out_shape=(shaped((1, n)), shaped((copies, 16 * basis.shape[0]))),
        in_specs=[whole()] * 7,
        out_specs=(whole(), whole()),
        compiler_params=params(),
        cost_estimate=pl.CostEstimate(
            flops=2 * n * k * 16, bytes_accessed=2 * n * k, transcendentals=0
        ),
    )(sketch, basis, own_image, *parts)


def add_kernel(rows_ref, copies_ref):
    total = jnp.sum(rows_ref[...], axis=0, keepdims=True)
    copies_ref[...] = jnp.broadcast_to(total, copies_ref.shape)


def add_and_copy(rows, copies):
    return pl.pallas_call(
        add_kernel,
        out_shape=shaped((copies, rows.shape[1])),
        in_specs=[whole()],
        out_specs=whole(),
        compiler_params=params(),
    )(rows)


def near_kernel(
    sketch_ref, far_ref, near_ref, mate_block_ref, token_ref, rows_in_ref, rows_ref, block_ref, sem
):
    del token_ref, rows_in_ref
    copy = column_copy(mate_block_ref, rows_ref, 1 + lax.axis_index("core"), sem)
    copy.start()
    rank, last = plane_rank()
    is_corner = (rank == 0) | (rank == last)

    left = jnp.where(is_corner, far_ref[...], sketch_ref[: block_ref.shape[0], :])
    block_ref[...] = dot_last(left, near_ref[...]).astype(BF16)

    copy.wait()


def near_block(sketch, far, near, mate_block, token, rows):
    n, k = near.shape
    return pl.pallas_call(
        near_kernel,
        out_shape=(shaped(rows.shape, rows.dtype), shaped((n, n), BF16)),
        in_specs=[whole()] * 5 + [whole(pl.ANY)],
        out_specs=(whole(pl.ANY), whole()),
        scratch_shapes=[pltpu.SemaphoreType.DMA],
        input_output_aliases={5: 0},
        compiler_params=params(),
        cost_estimate=pl.CostEstimate(
            flops=2 * n * n * k, bytes_accessed=4 * n * k, transcendentals=0
        ),
    )(sketch, far, near, mate_block, token, rows)


def far_kernel(sketch_ref, far_ref, near_block_ref, rows_in_ref, rows_ref, back_ref, block_ref, sem):
    del rows_in_ref
    copy = column_copy(near_block_ref, rows_ref, 2 - lax.axis_index("core"), sem)
    copy.start()
    back = dot_last(far_ref[...], sketch_ref[: back_ref.shape[0], :]).astype(BF16)
    back_ref[...] = back
    block_ref[...] = back.T
    copy.wait()


def far_blocks(sketch, far, near_block, rows):
    n, k = far.shape
    block = shaped((n, n), BF16)
    return pl.pallas_call(
        far_kernel,
        out_shape=(shaped(rows.shape, rows.dtype), block, block),
        in_specs=[whole()] * 3 + [whole(pl.ANY)],
        out_specs=(whole(pl.ANY), whole(), whole()),
        scratch_shapes=[pltpu.SemaphoreType.DMA],
        input_output_aliases={3: 0},
        compiler_params=params(),
        cost_estimate=pl.CostEstimate(
            flops=2 * n * n * k, bytes_accessed=4 * n * k, transcendentals=0
        ),
    )(sketch, far, near_block, rows)


def place_corner_kernel(corner_ref, rows_in_ref, rows_ref, sem):
    del rows_in_ref
    rank, last = plane_rank()

    @pl.when((rank == 0) | (rank == last))
    def _():
        copy = column_copy(corner_ref, rows_ref, 2 - lax.axis_index("core"), sem)
        copy.start()
        copy.wait()


def place_corner(corner, rows):
    return pl.pallas_call(
        place_corner_kernel,
        out_shape=shaped(rows.shape, rows.dtype),
        in_specs=[whole(), whole(pl.ANY)],
        out_specs=whole(pl.ANY),
        scratch_shapes=[pltpu.SemaphoreType.DMA],
        input_output_aliases={1: 0},
        compiler_params=params(),
        cost_estimate=pl.CostEstimate(flops=0, bytes_accessed=2 * corner.size, transcendentals=0),
    )(corner, rows)


def place_far_kernel(far_ref, back_ref, rows_in_ref, rows_ref, token_ref, sems):
    del rows_in_ref
    token_ref[...] = jnp.zeros_like(token_ref)
    core = lax.axis_index("core")
    far = column_copy(far_ref, rows_ref, 3 + core, sems.at[0])
    back = column_copy(back_ref, rows_ref, 4 - core, sems.at[1])
    far.start()
    back.start()
    far.wait()
    back.wait()


def place_far(far, back, rows):
    return pl.pallas_call(
        place_far_kernel,
        out_shape=(shaped(rows.shape, rows.dtype), shaped((8, 128))),
        in_specs=[whole()] * 2 + [whole(pl.ANY)],
        out_specs=(whole(pl.ANY), whole()),
        scratch_shapes=[pltpu.SemaphoreType.DMA((2,))],
        input_output_aliases={2: 0},
        compiler_params=params(),
        cost_estimate=pl.CostEstimate(flops=0, bytes_accessed=8 * far.size, transcendentals=0),
    )(far, back, rows)


def finish_kernel(count, sums_ref, basis_ref, image_ref, token_ref, left_ref, next_ref, stats_ref, lost_ref):
    del token_ref
    sums = jnp.sum(sums_ref[...], axis=0, keepdims=True)
    basis = basis_ref[...]
    m = basis.shape[0]
    shape = (m, sums.shape[1])
    line = lax.broadcasted_iota(jnp.int32, shape, 0)
    lane = lax.broadcasted_iota(jnp.int32, shape, 1)
    major, minor = lane // (2 * m), lane % (2 * m)
    spread = jnp.broadcast_to(sums, shape)
    inner = jnp.sum(jnp.where((major == line) & (minor == m), spread, 0.0), axis=1, keepdims=True)
    norm = jnp.sum(jnp.where(lane[0:1, :] == m + 1, sums, 0.0), axis=1, keepdims=True)
    coeffs = inner / count
    by_major = jnp.sum(jnp.where(major == line, coeffs, 0.0), axis=0, keepdims=True)
    by_minor = jnp.sum(jnp.where(minor == line, coeffs, 0.0), axis=0, keepdims=True)
    by_lane = jnp.sum(jnp.where(lane == line, coeffs, 0.0), axis=0, keepdims=True)
    quadratic = jnp.sum(sums * by_major * by_minor, axis=1, keepdims=True)
    cross = jnp.sum(coeffs * inner, axis=0, keepdims=True)
    square = (norm - cross) + (quadratic - cross)
    beta = jnp.sqrt(jnp.maximum(square, 0.0) / count + 1e-06)
    left = image_ref[...] - jnp.sum(coeffs * basis, axis=0, keepdims=True)
    left_ref[...] = left
    next_ref[...] = left / beta
    stats_ref[...] = jnp.where(lane[0:1, :] == m, beta, by_lane)
    largest = norm + cross + jnp.abs(quadratic)
    lost_ref[0] = jnp.max(jnp.where(square < 1e-3 * largest, 1.0, 0.0)).astype(jnp.int32)


def finish(sums, basis, image, count, token):
    row = shaped(image.shape)
    return pl.pallas_call(
        functools.partial(finish_kernel, count),
        out_shape=(row, row, shaped((1, 128)), shaped((1,), jnp.int32)),
        in_specs=[whole()] * 4,
        out_specs=(whole(), whole(), whole(), whole(pltpu.SMEM)),
        compiler_params=params(),
    )(sums, basis, image, token)


def group_size(group):
    members = 1
    for name in group:
        members *= lax.axis_size(name)
    return members


def on_device(sketch, basis):
    devices = group_size(AXES)
    stride = devices // SIZES[0]
    total_rows = basis.shape[1] * devices

    def move(block, source_of):
        return lax.ppermute(block, AXES, [(source_of(i) % devices, i) for i in range(devices)])

    def trade(rows, group):
        return lax.all_to_all(rows, group, 0, 0, tiled=True)

    def in_plane(i, step):
        return i // stride * stride + (i + step) % stride

    far = move(sketch, lambda i: i + stride if i % 2 == 0 else i - stride)
    near = move(sketch, lambda i: in_plane(i, -1 if i % 2 == 0 else 1))
    stored = [pltpu.with_memory_space_constraint(array, pltpu.HBM) for array in (sketch, basis)]
    sketch, u, basis = load_and_project(*stored)
    mate = move(sketch, lambda i: i ^ 1)
    mate_u, both_u = mate_projection(mate, u)
    far_u = move(both_u, lambda i: i - stride if i % 2 == 0 else i + stride)
    parts = (
        far_u,
        move(far_u, lambda i: i ^ 1),
        move(mate_u, lambda i: i - 2 if i % 2 == 0 else i + 2),
        mate_u,
    )
    rows, own_image, mate_block = own_blocks(sketch, mate, basis)
    image, sums = image_and_sums(sketch, basis, own_image, parts, group_size(FIRST_GROUP))
    sums = add_and_copy(trade(sums, FIRST_GROUP), group_size(SECOND_GROUP))
    rows, near = near_block(sketch, far, near, mate_block, sums, rows)
    rows, far_back, far_block = far_blocks(sketch, far, near, rows)
    def to_sender(i):
        return (i + stride if i % 2 == 0 else i - stride) % devices

    corners = [i for i in range(devices) if i % stride in (0, stride - 1)]
    corner = lax.ppermute(near, AXES, [(i, to_sender(i)) for i in corners] + [(2, 4)])
    far_back = lax.ppermute(far_back, AXES, [(i, to_sender(i)) for i in range(devices)])
    sums = trade(sums, SECOND_GROUP)
    rows = place_corner(corner, rows)
    rows, token = place_far(far_block, far_back, rows)
    left, next_vector, stats, lost = finish(sums, basis, image, float(total_rows), token)

    m = basis.shape[0]

    def from_sums():
        return next_vector[0], stats[0, : m + 1]

    def from_vector():
        square = lax.psum(jnp.sum(left * left), AXES)
        beta = jnp.sqrt(square / total_rows + 1e-06)
        return left[0] / beta, jnp.concatenate([stats[0, :m], beta[None]])

    next_vector, coefficients = lax.cond(lost[0] != 0, from_vector, from_sums)
    return rows, next_vector, coefficients


def solution(mesh):
    grid = Mesh(np.asarray(mesh.devices).reshape(SIZES), AXES)
    return jax.shard_map(
        on_device,
        mesh=grid,
        in_specs=(P(AXES, None), P(None, AXES)),
        out_specs=(P(AXES, None), P(AXES), P()),
        check_vma=False,
    )
```
